128 devices in a mesh: row: 8 (over z, x_hi), col: 16 (over y, x_lo, core).
Axes of the slice: x: 4 (x_hi: 2, x_lo: 2; x = x_hi * 2 + x_lo), y: 4, z: 4, core: 2. Of those that a mesh axis runs over, the one named last changes fastest.
Arguments:
- pages: float32 [16384, 1024], P(('row', 'col')), as said below
- transcripts: float32 [16384, 1024], P(('col', 'row')), as said below
- length_scale: float32 [1], replicated, may hold values from 0.6 to 0.9
Outputs:
- page_grad: float32 [16384, 1024], P(('row', 'col'))
- text_grad: float32 [16384, 1024], P(('col', 'row'))
The draws below stay inside these ranges and needn't reach their ends.
Inputs may be any that keep to these rules, and one draw needn't show every extreme that they name: `pages`: entries of page embeddings are finite and of magnitude at most 4. `transcripts`: entries of transcription embeddings are finite and of magnitude at most 4.
All inputs are finite; a program needn't handle non-finite values.
Results may differ from the reference program's by a relative error of at most 0.0003.
Values sent between devices are 32-bit elements; how exact they have to be, the bound alone decides.
No kernel may reach another device: no remote copies, remote signals or barrier semaphores. Data moves between devices by JAX's collectives and lax.ppermute only.
A program may use at most 128 MiB of HBM per device.

```python
import math
import jax
import jax.numpy as jnp
from jax import lax

D = 1024
X_DEV = 128
N = 16384
N_COL = 16


def draw_piece(key, shape, uniform_share):
    gauss_key, even_key = jax.random.split(key)
    gauss = jax.random.truncated_normal(gauss_key, -4.0, 4.0, shape, jnp.float32)
    even = jax.random.uniform(even_key, shape, jnp.float32, -1.7320508, 1.7320508)
    return uniform_share * even + (1.0 - uniform_share) * gauss


def column_mask(bounds):
    lower, upper, stride, offset = bounds
    count = sum((1 for column in range(lower, upper) if column % stride == offset))
    columns = jnp.arange(D)
    inside = (columns >= lower) & (columns < upper) & (columns % stride == offset)
    return inside.astype(jnp.float32) / math.sqrt(count)


def shared(key, groups, uniform_share, centre_bounds, item_bounds):
    keys = jax.random.split(key, 6)
    owners = jax.random.randint(keys[0], (N,), 0, groups)
    centres = 0.55 * draw_piece(keys[1], (groups, D), uniform_share) * column_mask(centre_bounds)[None, :]
    centres = centres + 0.85 * draw_piece(keys[2], (groups, D), uniform_share) / math.sqrt(D)
    items = 0.6 * draw_piece(keys[3], (N, D), uniform_share) * column_mask(item_bounds)[None, :]
    items = items + 0.3 * draw_piece(keys[4], (N, D), uniform_share) / math.sqrt(D)
    common = draw_piece(keys[5], (1, D), uniform_share) / math.sqrt(D)
    return (jnp.take(centres, owners, axis=0) + items, common)


def finish(key, centre_mean, common, uniform_share, common_weight, lowest, highest):
    noise_key, scale_key = jax.random.split(key)
    noise = 0.35 * draw_piece(noise_key, (N, D), uniform_share) / math.sqrt(D)
    scales = jnp.exp(jax.random.uniform(scale_key, (N, 1), jnp.float32, math.log(lowest), math.log(highest)))
    return (scales * (centre_mean + common_weight * common + noise)).astype(jnp.float32)


def draw_pages(key, part):
    centre_mean, common = shared(key, max(N // 64, 4), 0.0, (0, min(16, D), 1, 0), (min(16, D), min(48, D), 1, 0))
    key = jax.random.fold_in(key, 7)
    return finish(key, centre_mean, common, 0.0, 0.0, 0.6, 1.6)


def draw_transcripts(key, part):
    centre_mean, common = shared(key, max(N // 64, 4), 0.0, (0, min(16, D), 1, 0), (min(16, D), min(48, D), 1, 0))
    key = jax.random.fold_in(key, 13)
    return finish(key, centre_mean, common, 0.0, 0.0, 0.6, 1.6)


def setup_inputs(seed: int = 0) -> dict:
    splits = jax.random.split(jax.random.key(seed), 4)
    pages = draw_pages(jax.random.fold_in(splits[3], 71), 0)
    transcripts = draw_transcripts(jax.random.fold_in(splits[3], 71), 0)
    length_scale = jnp.clip(jax.random.uniform(splits[2], (1,), jnp.float32, 0.6, 0.9), 0.6, 0.9)
    return dict(pages=pages, transcripts=transcripts, length_scale=length_scale)


def kernel_tile(rows, cols, inverse):
    cross = lax.dot_general(rows, cols, (((1,), (1,)), ((), ())), precision=lax.Precision.HIGHEST, preferred_element_type=jnp.float32)
    first = lax.optimization_barrier(jnp.sum(rows * rows, axis=1))
    second = lax.optimization_barrier(jnp.sum(cols * cols, axis=1))
    return jnp.exp(-(first[:, None] + second[None, :] - 2.0 * cross) * inverse)

def reference(pages, transcripts, length_scale):
    spread_sq = length_scale[0] * length_scale[0]
    inverse = 0.5 / spread_sq
    height = X_DEV * N_COL
    blocks = N // height
    stacked = pages.reshape(blocks, height, D)
    starts = jnp.arange(blocks, dtype=jnp.int32) * height
    col_index = lax.iota(jnp.int32, N)

    def diag_mask(start):
        return ((start + lax.iota(jnp.int32, height))[:, None] == col_index[None, :]).astype(jnp.float32)

    def first_pass(carry, item):
        block, start = item
        kern = kernel_tile(block, transcripts, inverse)
        return (carry + lax.optimization_barrier(jnp.sum(kern, axis=0)), lax.optimization_barrier(jnp.sum(kern, axis=1)))
    col_sums, row_parts = lax.scan(first_pass, jnp.zeros((N,), jnp.float32), (stacked, starts))
    total = jnp.sum(row_parts)

    def centred_tile(block, rows):
        kern = kernel_tile(block, transcripts, inverse)
        centred = kern - rows[:, None] / N - col_sums[None, :] / N + total / (N * N)
        return (kern, centred)

    def second_pass(carry, item):
        block, start, rows = item
        kern, centred = centred_tile(block, rows)
        return ((carry[0] + jnp.sum(centred * centred), carry[1] + jnp.sum(centred * diag_mask(start))), None)
    zero = jnp.zeros((), jnp.float32)
    sums, unused = lax.scan(second_pass, (zero, zero), (stacked, starts, row_parts))
    frob_sq, align = sums
    frob = jnp.sqrt(frob_sq)
    loss_scale = 4.0 * N

    def third_pass(carry, item):
        block, start, rows = item
        kern, centred = centred_tile(block, rows)
        weight = (loss_scale * align / (frob * frob_sq) * centred - loss_scale / frob * (diag_mask(start) - 1.0 / N)) * kern
        mixed = jnp.dot(weight, transcripts, precision=lax.Precision.HIGHEST, preferred_element_type=jnp.float32)
        page_part = -(lax.optimization_barrier(jnp.sum(weight, axis=1))[:, None] * block - mixed) / spread_sq
        folded = lax.dot_general(weight, block, (((0,), (0,)), ((), ())), precision=lax.Precision.HIGHEST, preferred_element_type=jnp.float32)
        return ((carry[0] + folded, carry[1] + lax.optimization_barrier(jnp.sum(weight, axis=0))), page_part)
    init = (jnp.zeros((N, D), jnp.float32), jnp.zeros((N,), jnp.float32))
    accum, page_parts = lax.scan(third_pass, init, (stacked, starts, row_parts))
    text_grad = (accum[0] - accum[1][:, None] * transcripts) / spread_sq
    return (page_parts.reshape(N, D), text_grad)
```

```python
import jax
import jax.numpy as jnp
from jax import lax
from jax.sharding import Mesh, PartitionSpec as P

AXES = ("z", "xh", "y", "xl", "core")
SIZES = (4, 2, 4, 2, 2)
PRECISION = lax.Precision.HIGH


def from_next(x, axis, step):
    n = lax.axis_size(axis)
    return lax.ppermute(x, axis, [(i, (i - step) % n) for i in range(n)])


def from_twin(x):
    return lax.ppermute(x, ("xh", "xl"), [(0, 3), (3, 0), (1, 2), (2, 1)])


def from_side(x):
    return from_next(x, "xl", 1)


def from_core(x):
    return from_next(x, "core", 1)


def gather_ring(own, ring, across):
    half = own.shape[0] // 2
    other = across(own)
    up, down = from_next(own, ring, 1), from_next(own, ring, -1)
    o_up, o_down = from_next(other, ring, 1), from_next(other, ring, -1)
    far = jnp.concatenate([from_next(up[:half], ring, 1), from_next(down[half:], ring, -1)])
    o_far = across(far)
    return [[own, other], [up, o_up], [far, o_far], [down, o_down]]


def reduce_ring(parts, ring, across):
    (own, other), (up, o_up), (far, o_far), (down, o_down) = parts
    half = own.shape[0] // 2
    other = other + from_next(o_up, ring, -1) + from_next(o_down, ring, 1)
    far = far + across(o_far)
    own = own + across(other)
    low = from_next(far[:half], ring, -1)
    high = from_next(far[half:], ring, 1)
    up = jnp.concatenate([up[:half] + low, up[half:]])
    down = jnp.concatenate([down[:half], down[half:] + high])
    return own + from_next(up, ring, -1) + from_next(down, ring, 1)


def ring_total(v, ring):
    lead = v.shape[0]
    step = lead // 4
    out = v
    for e in (1, 2, 3):
        out = out + jnp.roll(from_next(v, ring, e), e * step, axis=0)
    return out


def flip(v, stride):
    shape = v.shape
    w = v.reshape(-1, 2, stride, shape[-1])
    return jnp.concatenate([w[:, 1:], w[:, :1]], axis=1).reshape(shape)


def kernel_tile(rows, cols, inverse):
    cross = lax.dot_general(
        rows, cols, (((1,), (1,)), ((), ())), precision=PRECISION, preferred_element_type=jnp.float32
    )
    first = jnp.sum(rows * rows, axis=1)
    second = jnp.sum(cols * cols, axis=1)
    return jnp.exp(-(first[:, None] + second[None, :] - 2.0 * cross) * inverse)


def merge_ring(mean, spread, weight, ring):
    means = [mean] + [from_next(mean, ring, e) for e in (1, 2, 3)]
    spreads = [spread] + [from_next(spread, ring, e) for e in (1, 2, 3)]
    return merge(means, spreads, weight)


def merge(means, spreads, weight):
    mean = sum(means) / len(means)
    return mean, sum(spreads) + weight * sum((m - mean) ** 2 for m in means), weight * len(means)


def on_device(pages, transcripts, length_scale):
    share = pages.shape[0]
    count = share * 128
    spread_sq = length_scale[0] * length_scale[0]
    inverse = 0.5 / spread_sq
    z, xh, y, xl, core = (lax.axis_index(a) for a in AXES)
    page_parts = gather_ring(pages, "y", from_side)
    page_list = []
    page_ids = []
    for dy in range(4):
        for dx in range(2):
            b = page_parts[dy][dx]
            page_list += [b, from_core(b)]
            for dc in range(2):
                page_ids.append((z * 2 + xh) * 16 + ((y + dy) % 4) * 4 + (xl ^ dx) * 2 + (core ^ dc))
    text_parts = gather_ring(transcripts, "z", from_twin)
    text_list = []
    text_ids = []
    for dz in range(4):
        for dq in range(2):
            text_list.append(text_parts[dz][dq])
            text_ids.append((y * 4 + (xl ^ dq) * 2 + core) * 8 + ((z + dz) % 4) * 2 + (xh ^ dq))
    page_block = jnp.concatenate(page_list)
    text_block = jnp.concatenate(text_list)
    kern = kernel_tile(page_block, text_block, inverse)
    lane = lax.iota(jnp.int32, share)
    row_glob = (jnp.stack(page_ids)[:, None] * share + lane[None, :]).reshape(-1)
    col_glob = (jnp.stack(text_ids)[:, None] * share + lane[None, :]).reshape(-1)
    on_diag = row_glob[:, None] == col_glob[None, :]
    row_sums = jnp.sum(kern, axis=1).reshape(16, share)
    col_sums = jnp.sum(kern, axis=0).reshape(8, share)
    row_sums = row_sums + flip(from_core(row_sums), 1)
    row_sums = row_sums + flip(from_side(row_sums), 2)
    row_sums = ring_total(row_sums, "y")
    col_sums = col_sums + flip(from_twin(col_sums), 1)
    col_sums = ring_total(col_sums, "z")
    rows = row_sums.reshape(-1) / count
    cols = col_sums.reshape(-1) / count
    rest = kern - rows[:, None] - cols[None, :]
    mean = jnp.mean(rest)
    spread = jnp.sum((rest - mean) ** 2)
    trace = jnp.sum(jnp.where(on_diag, rest, 0.0))
    weight = float(kern.size)
    line = jnp.stack([mean, spread, trace])
    stat = jnp.zeros((8, 128), jnp.float32).at[0, :3].set(line)

    def join(stats, weight):
        n = len(stats)
        total = sum(stats)
        mean = total[0, 0] / n
        extra = weight * sum((s[0, 0] - mean) ** 2 for s in stats)
        return total.at[0, 0].set(mean).at[0, 1].add(extra), weight * n

    stat, weight = join([stat, from_core(stat)], weight)
    stat, weight = join([stat, from_side(stat)], weight)
    stat, weight = join([stat] + [from_next(stat, "y", e) for e in (1, 2, 3)], weight)
    stat, weight = join([stat, from_next(stat, "xh", 1)], weight)
    stat, weight = join([stat] + [from_next(stat, "z", e) for e in (1, 2, 3)], weight)
    grand = -stat[0, 0]
    frob_sq = stat[0, 1]
    align = stat[0, 2] + count * grand
    frob = jnp.sqrt(frob_sq)
    loss_scale = 4.0 * count
    weights = (
        loss_scale * align / (frob * frob_sq) * (rest + grand)
        - loss_scale / frob * (on_diag.astype(jnp.float32) - 1.0 / count)
    ) * kern
    mixed = jnp.dot(weights, text_block, precision=PRECISION, preferred_element_type=jnp.float32)
    page_part = jnp.sum(weights, axis=1)[:, None] * page_block - mixed
    page_part = page_part.reshape(4, 2, 2, share, -1)
    folded = lax.dot_general(
        weights, page_block, (((0,), (0,)), ((), ())), precision=PRECISION, preferred_element_type=jnp.float32
    )
    text_part = folded - jnp.sum(weights, axis=0)[:, None] * text_block
    text_part = text_part.reshape(4, 2, share, -1)
    page_sum = reduce_ring(
        [[page_part[dy, dx, 0] + from_core(page_part[dy, dx, 1]) for dx in range(2)] for dy in range(4)],
        "y",
        from_side,
    )
    text_sum = reduce_ring([[text_part[dz, dq] for dq in range(2)] for dz in range(4)], "z", from_twin)
    return (-page_sum / spread_sq, text_sum / spread_sq)


def solution(mesh):
    grid = Mesh(mesh.devices.reshape(SIZES), AXES)
    row, col = ("z", "xh"), ("y", "xl", "core")
    placed = (P(row + col, None), P(col + row, None), P())
    return jax.shard_map(
        on_device,
        mesh=grid,
        in_specs=placed,
        out_specs=(P(row + col, None), P(col + row, None)),
        check_vma=False,
    )
```

```python
import functools

import jax
import jax.numpy as jnp
from jax import lax
from jax.experimental import pallas as pl
from jax.experimental.pallas import tpu as pltpu
from jax.sharding import Mesh, PartitionSpec as P

AXES = ("z", "xh", "y", "xl", "core")
SIZES = (4, 2, 4, 2, 2)
COUNT = 16384
HEIGHT, WIDTH, DEPTH, SHARE = 2048, 1024, 1024, 128
F32, BF16 = jnp.float32, jnp.bfloat16
WHOLE = pl.BlockSpec(memory_space=pltpu.VMEM)
SCALAR = pl.BlockSpec(memory_space=pltpu.SMEM)
VMEM_BYTES = 20 * 2**20
NT = (((1,), (1,)), ((), ()))
NN = (((1,), (0,)), ((), ()))
TN = (((0,), (0,)), ((), ()))


def from_next(x, axis, step):
    n = lax.axis_size(axis)
    return lax.ppermute(x, axis, [(i, (i - step) % n) for i in range(n)])


def from_twin(x):
    return lax.ppermute(x, ("xh", "xl"), [(0, 3), (3, 0), (1, 2), (2, 1)])


def from_side(x):
    return from_next(x, "xl", 1)


def from_core(x):
    return from_next(x, "core", 1)


def together(*values):
    return lax.optimization_barrier(values)


def gather(pages, texts):
    half = pages.shape[0] // 2
    (p_side, p_up, p_down, t_side, t_up, t_down) = together(
        from_side(pages),
        from_next(pages, "y", 1),
        from_next(pages, "y", -1),
        from_twin(texts),
        from_next(texts, "z", 1),
        from_next(texts, "z", -1),
    )
    p_low, p_high, t_low, t_high = together(
        from_next(p_up[:half], "y", 1),
        from_next(p_down[half:], "y", -1),
        from_next(t_up[:half], "z", 1),
        from_next(t_down[half:], "z", -1),
    )
    p_far = jnp.concatenate([p_low, p_high])
    t_far = jnp.concatenate([t_low, t_high])
    p_side2, t_side2, p_far2, t_far2 = together(p_side, t_side, p_far, t_far)
    (sp_up, sp_down, sp_far, st_up, st_down, st_far) = (
        from_next(p_side2, "y", 1),
        from_next(p_side2, "y", -1),
        from_side(p_far2),
        from_next(t_side2, "z", 1),
        from_next(t_side2, "z", -1),
        from_twin(t_far2),
    )
    return (
        [pages, p_up, p_far, p_down, p_side, sp_up, sp_far, sp_down],
        [texts, t_up, t_far, t_down, t_side, st_up, st_far, st_down],
    )


def scatter(p, t):
    half = p[0].shape[0] // 2
    py1, py2, px, tz1, tz2, tx = together(
        from_next(p[5], "y", -1),
        from_next(p[7], "y", 1),
        from_side(p[6]),
        from_next(t[5], "z", -1),
        from_next(t[7], "z", 1),
        from_twin(t[6]),
    )
    p_far, t_far = p[2] + px, t[2] + tx
    p_side, t_side = p[4] + py1 + py2, t[4] + tz1 + tz2
    p_low, p_high, t_low, t_high = together(
        from_next(p_far[:half], "y", -1),
        from_next(p_far[half:], "y", 1),
        from_next(t_far[:half], "z", -1),
        from_next(t_far[half:], "z", 1),
    )
    p_up = jnp.concatenate([p[1][:half] + p_low, p[1][half:]])
    p_down = jnp.concatenate([p[3][:half], p[3][half:] + p_high])
    t_up = jnp.concatenate([t[1][:half] + t_low, t[1][half:]])
    t_down = jnp.concatenate([t[3][:half], t[3][half:] + t_high])
    got = together(
        from_next(p_up, "y", -1),
        from_next(p_down, "y", 1),
        from_side(p_side),
        from_next(t_up, "z", -1),
        from_next(t_down, "z", 1),
        from_twin(t_side),
    )
    return p[0] + got[0] + got[1] + got[2], t[0] + got[3] + got[4] + got[5]


def split(x):
    high = x.astype(BF16)
    return high, (x - high.astype(F32)).astype(BF16)


def fold(x):
    return functools.reduce(jnp.add, [x[:, i : i + 128] for i in range(0, x.shape[1], 128)])


def as_lanes(x):
    return jnp.sum(jnp.transpose(fold(x)), axis=0, keepdims=True)


def as_column(line):
    return jnp.transpose(jnp.broadcast_to(line, (128, 128)))


def dot3(ah, al, bh, bl, dims):
    d = functools.partial(lax.dot_general, dimension_numbers=dims, preferred_element_type=F32)
    return d(ah, bh) + (d(ah, bl) + d(al, bh))


CHUNK = 512


def cross_kernel(*refs):
    inverse_ref, row_ids, col_ids = refs[:3]
    pages, texts = refs[3:19], refs[19:27]
    kern, ph, pl_, th, tl, rows, cols = refs[27:34]
    pnorm, tnorm, col_acc, ident = refs[34:]
    inverse = inverse_ref[0]
    for b in range(8):
        t = texts[b][...]
        cut = pl.ds(b * 128, 128)
        th[cut, :], tl[cut, :] = split(t)
        tnorm[:, cut] = as_lanes(t * t)
    for b in range(16):
        p = pages[b][...]
        cut = pl.ds(b * 128, 128)
        ph[cut, :], pl_[cut, :] = split(p)
        pnorm[cut, :] = jnp.broadcast_to(jnp.sum(p * p, axis=1, keepdims=True), (128, 128))
    col_acc[...] = jnp.zeros_like(col_acc)
    rows[...] = jnp.zeros_like(rows)
    cols[...] = jnp.zeros_like(cols)

    @pl.loop(0, 2048 // CHUNK)
    def _(c):
        start = pl.multiple_of(c * CHUNK, CHUNK)
        cut = pl.ds(start, CHUNK)
        cross = dot3(ph[cut, :], pl_[cut, :], th[...], tl[...], NT)
        k = jnp.exp((2.0 * cross - pnorm[cut, :1] - tnorm[...]) * inverse)
        kern[cut, :] = k
        col_acc[...] += jnp.sum(k.reshape(CHUNK // 8, 8, 1024), axis=0)
        lines = [as_lanes(k[i : i + 128]) for i in range(0, CHUNK, 128)]
        for i in range(CHUNK // 128):
            rows[pl.ds(c * (CHUNK // 128) + i, 1), :] = lines[i]

    total = jnp.sum(col_acc[...], axis=0, keepdims=True)
    for b in range(8):
        cols[b : b + 1, :] = total[:, b * 128 : b * 128 + 128]
        ident[:, b * 128 : b * 128 + 128] = lax.broadcasted_iota(jnp.int32, (1, 128), 1) + col_ids[b] * 128
    tile_mean = jnp.sum(total) / (2048.0 * 1024.0)
    shift = total / 2048.0 - tile_mean

    def stat(b, carry):
        inner, trace = carry
        cut = pl.ds(pl.multiple_of(b * 128, 128), 128)
        k = kern[cut, :]
        mean = as_column(rows[pl.ds(b, 1), :] / 1024.0)[:, :1]
        own = k - mean - shift
        here = (lax.broadcasted_iota(jnp.int32, (128, 1), 0) + row_ids[b] * 128) == ident[...]
        diag = jnp.where(here, k, 0.0)
        inner = inner + jnp.sum(fold(own * own).reshape(16, 8, 128), axis=0)
        trace = trace + jnp.sum(fold(diag).reshape(16, 8, 128), axis=0)
        return inner, trace

    zero = jnp.zeros((8, 128), F32)
    inner, trace = lax.fori_loop(0, 16, stat, (zero, zero))
    rows[16:17, :] = jnp.sum(inner, axis=0, keepdims=True)
    rows[17:18, :] = jnp.sum(trace, axis=0, keepdims=True)


def cross(inverse, row_ids, col_ids, pages, texts):
    out = [
        pltpu.VMEM((HEIGHT, WIDTH), F32),
        pltpu.VMEM((HEIGHT, DEPTH), BF16),
        pltpu.VMEM((HEIGHT, DEPTH), BF16),
        pltpu.VMEM((WIDTH, DEPTH), BF16),
        pltpu.VMEM((WIDTH, DEPTH), BF16),
        jax.ShapeDtypeStruct((24, 128), F32),
        jax.ShapeDtypeStruct((16, 128), F32),
    ]
    return pl.pallas_call(
        cross_kernel,
        out_shape=out,
        in_specs=[SCALAR] * 3 + [WHOLE] * 24,
        out_specs=[WHOLE] * 7,
        scratch_shapes=[
            pltpu.VMEM((2048, 128), F32),
            pltpu.VMEM((1, 1024), F32),
            pltpu.VMEM((8, 1024), F32),
            pltpu.VMEM((1, 1024), jnp.int32),
        ],
        compiler_params=pltpu.CompilerParams(vmem_limit_bytes=VMEM_BYTES),
        cost_estimate=pl.CostEstimate(flops=3 * 2 * 2**31, bytes_accessed=32 * 2**20, transcendentals=2**21),
        name="cross",
    )(inverse, row_ids, col_ids, *pages, *texts)

def page_kernel(*refs):
    facts, row_ids, col_ids, kern, ph, pl_, th, tl, rows, cols = refs[:10]
    outs = refs[10:26]
    wh, wl, heavy = refs[26:29]
    mean_t, ident = refs[29:]
    per_row = 1.0 / COUNT
    slope, base, spike = facts[0:1, :1], facts[1:2, :1], facts[2:3, :1]
    for b in range(8):
        mean_t[:, b * 128 : b * 128 + 128] = cols[b : b + 1, :] * per_row
        ident[:, b * 128 : b * 128 + 128] = lax.broadcasted_iota(jnp.int32, (1, 128), 1) + col_ids[b] * 128
    acc = jnp.zeros((8, 1024), F32)
    n = 512
    for b in range(0, 2048, n):
        cut = pl.ds(b, n)
        k = kern[cut, :]
        r = jnp.concatenate([as_column(rows[i : i + 1, :] * per_row) for i in range(b // 128, (b + n) // 128)])[:, :1]
        g = jnp.concatenate([lax.broadcasted_iota(jnp.int32, (128, 1), 0) + row_ids[i] * 128 for i in range(b // 128, (b + n) // 128)])
        w = (slope * (k - r - mean_t[...]) + jnp.where(g == ident[...], base - spike, base)) * k
        h, l = split(w)
        wh[cut, :] = h
        wl[cut, :] = l
        acc = acc + jnp.sum(w.reshape(n // 8, 8, 1024), axis=0)
        mixed = dot3(h, l, th[...], tl[...], NN)
        load = jnp.sum(w, axis=1, keepdims=True)
        p = ph[cut, :].astype(F32) + pl_[cut, :].astype(F32)
        g = load * p - mixed
        for i in range(n // 128):
            outs[b // 128 + i][...] = g[i * 128 : i * 128 + 128]
    heavy[...] = acc


def page_part(facts, row_ids, col_ids, kern, ph, pl_, th, tl, rows, cols):
    return pl.pallas_call(
        page_kernel,
        out_shape=[pltpu.VMEM((128, 1024), F32)] * 16
        + [pltpu.VMEM((2048, 1024), BF16), pltpu.VMEM((2048, 1024), BF16), jax.ShapeDtypeStruct((8, 1024), F32)],
        in_specs=[WHOLE] + [SCALAR] * 2 + [WHOLE] * 7,
        out_specs=[WHOLE] * 19,
        scratch_shapes=[pltpu.VMEM((1, 1024), F32), pltpu.VMEM((1, 1024), jnp.int32)],
        compiler_params=pltpu.CompilerParams(vmem_limit_bytes=VMEM_BYTES),
        cost_estimate=pl.CostEstimate(flops=3 * 2 * 2**31, bytes_accessed=32 * 2**20, transcendentals=0),
        name="page_part",
    )(facts, row_ids, col_ids, kern, ph, pl_, th, tl, rows, cols)


TN = (((0,), (0,)), ((), ()))
def text_kernel(*refs):
    wh, wl, ph, pl_, th, tl, heavy = refs[:7]
    outs = refs[7:15]
    load = jnp.sum(heavy[...], axis=0, keepdims=True)
    for j in range(0, 1024, 256):
        folded = dot3(wh[:, j:j+256], wl[:, j:j+256], ph[...], pl_[...], TN)
        for i in range(2):
            q=j+i*128
            col = as_column(load[:, q : q + 128])[:, :1]
            t = th[q : q + 128, :].astype(F32) + tl[q : q + 128, :].astype(F32)
            outs[q//128][...] = folded[i*128:i*128+128] - col * t


def text_part(wh, wl, ph, pl_, th, tl, heavy):
    return pl.pallas_call(
        text_kernel,
        out_shape=[pltpu.VMEM((128, 1024), F32)] * 8,
        in_specs=[WHOLE] * 7,
        out_specs=[WHOLE] * 8,
        compiler_params=pltpu.CompilerParams(vmem_limit_bytes=VMEM_BYTES),
        cost_estimate=pl.CostEstimate(flops=3 * 2 * 2**31, bytes_accessed=32 * 2**20, transcendentals=0),
        name="text_part",
    )(wh, wl, ph, pl_, th, tl, heavy)


def swap(x, step):
    parts = [x[i : i + step] for i in range(0, x.shape[0], step)]
    order = [j for i in range(0, len(parts), 2) for j in (i + 1, i)]
    return jnp.concatenate([parts[j] for j in order])


def turn(x, e):
    runs = [x[i : i + 4] for i in range(0, x.shape[0], 4)]
    return jnp.concatenate([piece for r in runs for piece in (r[4 - e :], r[: 4 - e])])


def line_sum(x):
    return jnp.sum(x, axis=0, keepdims=True)


def without_mean(x):
    return x - jnp.mean(x)


def first_merge(r, r_side, c, c_twin, r_out, c_out):
    a, b = r[:16], swap(r_side[:16], 4)
    d = a - b
    r_out[:16] = a + b
    r_out[16:] = r[16:] + r_side[16:]
    r_out[16:17] += line_sum(d * d) / (2.0 * WIDTH)
    a, b = c[:8], swap(c_twin[:8], 4)
    d = without_mean(a - b)
    c_out[:8] = a + b
    c_out[8:] = c[8:] + c_twin[8:]
    c_out[8:9] += line_sum(d * d) / (2.0 * HEIGHT)


def second_merge(r, r1, r2, r3, c, c1, c2, c3, r_out, c_out):
    parts = [r[:16]] + [turn(g[:16], e) for e, g in ((1, r1), (2, r2), (3, r3))]
    total = parts[0] + parts[1] + parts[2] + parts[3]
    r_out[:16] = total
    r_out[16:] = r[16:] + r1[16:] + r2[16:] + r3[16:]
    for part in parts:
        d = part - 0.25 * total
        r_out[16:17] += line_sum(d * d) / (2.0 * WIDTH)
    parts = [c[:8]] + [turn(g[:8], e) for e, g in ((1, c1), (2, c2), (3, c3))]
    total = parts[0] + parts[1] + parts[2] + parts[3]
    c_out[:8] = total
    c_out[8:] = c[8:] + c1[8:] + c2[8:] + c3[8:]
    for part in parts:
        d = without_mean(part - 0.25 * total)
        c_out[8:9] += line_sum(d * d) / (2.0 * HEIGHT)


def third_merge(r, r_core, c, r_out, s_out, u_out):
    a, b = r[:16], swap(r_core[:16], 8)
    d = a - b
    both = a + b
    r_out[...] = both
    s_out[...] = jnp.zeros_like(s_out)
    s_out[0:1] = r[16:17] + r_core[16:17] + line_sum(d * d) / (16.0 * WIDTH)
    s_out[1:2] = r[17:18] + r_core[17:18]
    s_out[2:3] = line_sum(both)
    u_out[...] = jnp.zeros_like(u_out)
    u_out[0:1] = c[8:9]
    u_out[1:2] = jnp.broadcast_to(jnp.sum(c[:8]).reshape(1, 1), (1, 128))


def fourth_merge(s, s_twin, u, u_side, s_out, u_out):
    s_out[...] = s[...] + s_twin[...]
    d = u[1:2] - u_side[1:2]
    u_out[...] = u[...] + u_side[...]
    u_out[2:3] += d * d / 2.0


def fifth_merge(s, s1, s2, s3, u, u1, u2, u3, s_out, u_out):
    s_out[...] = s[...] + s1[...] + s2[...] + s3[...]
    total = u[...] + u1[...] + u2[...] + u3[...]
    u_out[...] = total
    for part in (u, u1, u2, u3):
        d = part[1:2] - 0.25 * total[1:2]
        u_out[2:3] += d * d / 2.0


def last_merge(s, u, u_core, facts):
    def whole(line):
        return jnp.broadcast_to(jnp.sum(line).reshape(1, 1), (1, 128))

    d = u[1:2] - u_core[1:2]
    offset = u[2:3] + u_core[2:3] + d * d / 16.0
    total = whole(s[2:3])
    frob_sq = whole(s[0:1] + u[0:1] + u_core[0:1]) - offset / (COUNT * float(WIDTH))
    align = whole(s[1:2]) - total / COUNT
    grand = total / (float(COUNT) * COUNT)
    spike = 4.0 * COUNT / jnp.sqrt(frob_sq)
    slope = spike * (align / frob_sq)
    facts[...] = jnp.zeros_like(facts)
    facts[0:1] = slope
    facts[1:2] = slope * grand + spike / COUNT
    facts[2:3] = spike


def small(body, shapes, *args):
    return pl.pallas_call(
        body,
        out_shape=[jax.ShapeDtypeStruct(s, F32) for s in shapes],
        in_specs=[WHOLE] * len(args),
        out_specs=[WHOLE] * len(shapes),
        cost_estimate=pl.CostEstimate(flops=10000, bytes_accessed=100000, transcendentals=0),
        name=body.__name__,
    )(*args)


def ring(x, axis):
    return [from_next(x, axis, e) for e in (1, 2, 3)]


def statistics(r, c):
    big, mid, one = (24, 128), (16, 128), (8, 128)
    r, c = small(first_merge, [big, mid], r, from_side(r), c, from_twin(c))
    r, c = small(second_merge, [big, mid], r, *ring(r, "y"), c, *ring(c, "z"))
    r, s, u = small(third_merge, [mid, one, one], r, from_core(r), c)
    s, u = small(fourth_merge, [one, one], s, from_twin(s), u, from_side(u))
    s, u = small(fifth_merge, [one, one], s, *ring(s, "z"), u, *ring(u, "y"))
    (facts,) = small(last_merge, [one], s, u, from_core(u))
    return r, c, facts


def on_device(pages, transcripts, length_scale):
    spread_sq = length_scale[0] * length_scale[0]
    inverse = 0.5 / spread_sq
    z, xh, y, xl, core = (lax.axis_index(a) for a in AXES)
    near, texts = gather(pages, transcripts)
    blocks = near + [from_core(b) for b in near]
    row_ids = jnp.stack(
        [
            (z * 2 + xh) * 16 + ((y + dy) % 4) * 4 + (xl ^ dx) * 2 + (core ^ dc)
            for dc in range(2)
            for dx in range(2)
            for dy in range(4)
        ]
    )
    col_ids = jnp.stack(
        [
            (y * 4 + (xl ^ dq) * 2 + core) * 8 + ((z + dz) % 4) * 2 + (xh ^ dq)
            for dq in range(2)
            for dz in range(4)
        ]
    )
    kern, ph, pl_, th, tl, r, c = cross(inverse.reshape(1), row_ids, col_ids, blocks, texts)
    r, c, facts = statistics(r, c)
    got = page_part(facts, row_ids, col_ids, kern, ph, pl_, th, tl, r, c)
    text_sums = text_part(got[16], got[17], ph, pl_, th, tl, got[18])
    page_sums = [got[i] + from_core(got[8 + i]) for i in range(8)]
    page_sum, text_sum = scatter(page_sums, text_sums)
    return (-page_sum / spread_sq, text_sum / spread_sq)


def solution(mesh):
    grid = Mesh(mesh.devices.reshape(SIZES), AXES)
    row, col = ("z", "xh"), ("y", "xl", "core")
    placed = (P(row + col, None), P(col + row, None), P())
    return jax.shard_map(
        on_device,
        mesh=grid,
        in_specs=placed,
        out_specs=(P(row + col, None), P(col + row, None)),
        check_vma=False,
    )
```

```python
import functools

import jax
import jax.numpy as jnp
from jax import lax
from jax.experimental import pallas as pl
from jax.experimental.pallas import tpu as pltpu
from jax.sharding import Mesh, PartitionSpec as P

AXES = ("z", "xh", "y", "xl", "core")
SIZES = (4, 2, 4, 2, 2)
COUNT = 16384
HEIGHT, WIDTH, DEPTH, SHARE = 2048, 1024, 1024, 128
F32, BF16 = jnp.float32, jnp.bfloat16
WHOLE = pl.BlockSpec(memory_space=pltpu.VMEM)
SCALAR = pl.BlockSpec(memory_space=pltpu.SMEM)
NT = (((1,), (1,)), ((), ()))
NN = (((1,), (0,)), ((), ()))
TN = (((0,), (0,)), ((), ()))


def from_next(x, axis, step):
    n = lax.axis_size(axis)
    return lax.ppermute(x, axis, [(i, (i - step) % n) for i in range(n)])


def from_twin(x):
    return lax.ppermute(x, ("xh", "xl"), [(0, 3), (3, 0), (1, 2), (2, 1)])


def from_side(x):
    return from_next(x, "xl", 1)


def from_core(x):
    return from_next(x, "core", 1)


def together(*values):
    return lax.optimization_barrier(values)


def gather(texts):
    half = texts.shape[0] // 2
    side, up, down = together(from_twin(texts), from_next(texts, "z", 1), from_next(texts, "z", -1))
    low, high = together(from_next(up[:half], "z", 1), from_next(down[half:], "z", -1))
    far = jnp.concatenate([low, high])
    side2, far2 = together(side, far)
    return [
        texts, up, far, down,
        side, from_next(side2, "z", 1), from_twin(far2), from_next(side2, "z", -1),
    ]


class Ring:
    def __init__(self, axis, across):
        self.axis, self.across = axis, across

    def first(self, o_up, o_down, o_far):
        self.got = (from_next(o_up, self.axis, -1), from_next(o_down, self.axis, 1), self.across(o_far))

    def second(self, far, other):
        low, high, o_far = self.got
        far = far + o_far
        half = far.shape[0] // 2
        self.halves = (from_next(far[:half], self.axis, -1), from_next(far[half:], self.axis, 1))
        self.other = self.across(other + low + high)

    def third(self, own, up, down):
        half = own.shape[0] // 2
        low, high = self.halves
        up = jnp.concatenate([up[:half] + low, up[half:]])
        down = jnp.concatenate([down[:half], down[half:] + high])
        return own + from_next(up, self.axis, -1) + from_next(down, self.axis, 1) + self.other


def split(x):
    high = x.astype(BF16)
    return high, (x - high.astype(F32)).astype(BF16)


def fold(x):
    return functools.reduce(jnp.add, [x[:, i : i + 128] for i in range(0, x.shape[1], 128)])


def as_lanes(x):
    return jnp.sum(jnp.transpose(fold(x)), axis=0, keepdims=True)


def as_column(line):
    return jnp.transpose(jnp.broadcast_to(line, (128, 128)))


def dot3(ah, al, bh, bl, dims):
    d = functools.partial(lax.dot_general, dimension_numbers=dims, preferred_element_type=F32)
    return d(ah, bh) + (d(ah, bl) + d(al, bh))


CHUNK = 512
CHUNKS = HEIGHT // CHUNK
HBM = pl.BlockSpec(memory_space=pltpu.HBM)


def text_split_kernel(*refs):
    texts = refs[:8]
    tnorm, th_out, tl_out, th, tl, sem = refs[8:]
    for b in range(8):
        t = texts[b][...]
        cut = pl.ds(b * 128, 128)
        th[cut, :], tl[cut, :] = split(t)
        tnorm[:, b * 128 : b * 128 + 128] = as_lanes(t * t)
    high = pltpu.make_async_copy(th, th_out, sem.at[0])
    low = pltpu.make_async_copy(tl, tl_out, sem.at[1])
    high.start()
    low.start()
    high.wait()
    low.wait()


def text_split(texts):
    return pl.pallas_call(
        text_split_kernel,
        out_shape=[jax.ShapeDtypeStruct((1, WIDTH), F32)] + [pltpu.HBM((WIDTH, DEPTH), BF16)] * 2,
        in_specs=[WHOLE] * 8,
        out_specs=[WHOLE] + [HBM] * 2,
        scratch_shapes=[pltpu.VMEM((WIDTH, DEPTH), BF16)] * 2 + [pltpu.SemaphoreType.DMA((2,))],
        compiler_params=pltpu.CompilerParams(vmem_limit_bytes=14 * 2**20),
        cost_estimate=pl.CostEstimate(flops=2**24, bytes_accessed=8 * 2**20, transcendentals=0),
        name="text_split",
    )(*texts)


def cross_kernel(
    inverse_ref, row_ids, col_ids, pages, th_in, tl_in, tnorm,
    kern, ph, pl_, rows, cols,
    page_in, held, high, low, th, tl, col_acc, ident, in_sem, out_sem, text_sem,
):
    inverse = inverse_ref[0]

    def page_copy(c):
        return pltpu.make_async_copy(pages.at[pl.ds(c * CHUNK, CHUNK), :], page_in.at[c % 2], in_sem.at[c])

    def out_copies(c):
        cut = pl.ds(c * CHUNK, CHUNK)
        return (
            pltpu.make_async_copy(high.at[c % 2], ph.at[cut, :], out_sem.at[0, c]),
            pltpu.make_async_copy(low.at[c % 2], pl_.at[cut, :], out_sem.at[1, c]),
            pltpu.make_async_copy(held.at[cut, :], kern.at[cut, :], out_sem.at[2, c]),
        )

    text_copies = (
        pltpu.make_async_copy(th_in, th, text_sem.at[0]),
        pltpu.make_async_copy(tl_in, tl, text_sem.at[1]),
    )
    page_copy(0).start()
    for copy in text_copies:
        copy.start()
    page_copy(1).start()
    col_acc[...] = jnp.zeros_like(col_acc)
    rows[...] = jnp.zeros_like(rows)
    cols[...] = jnp.zeros_like(cols)
    for c in range(CHUNKS):
        page_copy(c).wait()
        h_copy, l_copy, k_copy = out_copies(c)
        if c >= 2:
            for copy in out_copies(c - 2)[:2]:
                copy.wait()
        p = page_in[c % 2]
        high[c % 2], low[c % 2] = split(p)
        pnorm = jnp.sum(p * p, axis=1, keepdims=True)
        h_copy.start()
        l_copy.start()
        if c + 2 < CHUNKS:
            page_copy(c + 2).start()
        if c == 0:
            for copy in text_copies:
                copy.wait()
        cross = dot3(high[c % 2], low[c % 2], th[...], tl[...], NT)
        k = jnp.exp((2.0 * cross - pnorm - tnorm[...]) * inverse)
        held[c * CHUNK : c * CHUNK + CHUNK, :] = k
        k_copy.start()
        col_acc[...] += jnp.sum(k.reshape(CHUNK // 8, 8, WIDTH), axis=0)
        for i in range(0, CHUNK, 128):
            line = (c * CHUNK + i) // 128
            rows[line : line + 1, :] = as_lanes(k[i : i + 128])

    total = jnp.sum(col_acc[...], axis=0, keepdims=True)
    for b in range(8):
        cols[pl.ds(col_ids[b] & 7, 1), :] = total[:, b * 128 : b * 128 + 128]
        ident[:, b * 128 : b * 128 + 128] = lax.broadcasted_iota(jnp.int32, (1, 128), 1) + col_ids[b] * 128
    tile_mean = jnp.sum(total) / (float(HEIGHT) * WIDTH)
    shift = total / float(HEIGHT) - tile_mean

    def stat(b, carry):
        inner, trace = carry
        k = held[pl.ds(pl.multiple_of(b * 128, 128), 128), :]
        mean = as_column(rows[pl.ds(b, 1), :] / float(WIDTH))[:, :1]
        own = k - mean - shift
        here = (lax.broadcasted_iota(jnp.int32, (128, 1), 0) + row_ids[b] * 128) == ident[...]
        diag = jnp.where(here, k, 0.0)
        inner = inner + jnp.sum(fold(own * own).reshape(16, 8, 128), axis=0)
        trace = trace + jnp.sum(fold(diag).reshape(16, 8, 128), axis=0)
        return inner, trace

    zero = jnp.zeros((8, 128), F32)
    inner, trace = lax.fori_loop(0, 16, stat, (zero, zero))
    rows[16:17, :] = jnp.sum(inner, axis=0, keepdims=True)
    rows[17:18, :] = jnp.sum(trace, axis=0, keepdims=True)
    for c in range(CHUNKS):
        for copy in out_copies(c)[0 if c >= CHUNKS - 2 else 2 :]:
            copy.wait()


def cross(inverse, row_ids, col_ids, pages, th, tl, tnorm):
    return pl.pallas_call(
        cross_kernel,
        out_shape=[
            pltpu.HBM((HEIGHT, WIDTH), F32),
            pltpu.HBM((HEIGHT, DEPTH), BF16),
            pltpu.HBM((HEIGHT, DEPTH), BF16),
            jax.ShapeDtypeStruct((24, 128), F32),
            jax.ShapeDtypeStruct((16, 128), F32),
        ],
        in_specs=[SCALAR] * 3 + [HBM] * 3 + [WHOLE],
        out_specs=[HBM] * 3 + [WHOLE] * 2,
        scratch_shapes=[
            pltpu.VMEM((2, CHUNK, DEPTH), F32),
            pltpu.VMEM((HEIGHT, WIDTH), F32),
            pltpu.VMEM((2, CHUNK, DEPTH), BF16),
            pltpu.VMEM((2, CHUNK, DEPTH), BF16),
            pltpu.VMEM((WIDTH, DEPTH), BF16),
            pltpu.VMEM((WIDTH, DEPTH), BF16),
            pltpu.VMEM((8, WIDTH), F32),
            pltpu.VMEM((1, WIDTH), jnp.int32),
            pltpu.SemaphoreType.DMA((CHUNKS,)),
            pltpu.SemaphoreType.DMA((3, CHUNKS)),
            pltpu.SemaphoreType.DMA((2,)),
        ],
        compiler_params=pltpu.CompilerParams(vmem_limit_bytes=36 * 2**20),
        cost_estimate=pl.CostEstimate(flops=6 * 2**31, bytes_accessed=8 * 2**20, transcendentals=2**21),
        name="cross",
    )(inverse, row_ids, col_ids, afar(pages), afar(th), afar(tl), tnorm)


def afar(x):
    return pltpu.with_memory_space_constraint(x, pltpu.HBM)


def near(x):
    return pltpu.with_memory_space_constraint(x, pltpu.VMEM)


def page_blocks(places, outs, wh, wl, load, ph, pl_, th, tl, size):
    for first in range(0, len(outs), size):
        cuts = [pl.ds(pl.multiple_of(p * 128, 128), 128) for p in places[first : first + size]]
        high = jnp.concatenate([wh[c, :] for c in cuts])
        low = jnp.concatenate([wl[c, :] for c in cuts])
        mixed = dot3(high, low, th[...], tl[...], NN)
        for i, c in enumerate(cuts):
            p = ph[c, :].astype(F32) + pl_[c, :].astype(F32)
            outs[first + i][...] = load[c, :1] * p - mixed[i * 128 : i * 128 + 128]


FIRST = (5, 7, 6, 2, 4, 13, 15, 14, 10, 12)
SECOND = (1, 3, 0, 9, 11, 8)
STEP = 256


def weight_kernel(*refs):
    facts, row_ids, col_ids, order, kern, ph_in, pl_in, th_in, tl_in, rows, cols = refs[:11]
    outs = refs[11:21]
    wh, wl, load, heavy, ph, pl_, th, tl = refs[21:29]
    mean_t, ident, held, k_sem, in_sem = refs[29:]
    k_copies = [
        pltpu.make_async_copy(kern.at[pl.ds(b, STEP), :], held.at[pl.ds(b, STEP), :], k_sem.at[b // STEP])
        for b in range(0, HEIGHT, STEP)
    ]
    copies = [
        pltpu.make_async_copy(src, dst, in_sem.at[i])
        for i, (src, dst) in enumerate(((th_in, th), (tl_in, tl), (ph_in, ph), (pl_in, pl_)))
    ]
    for copy in k_copies + copies:
        copy.start()
    per_row = 1.0 / COUNT
    slope, base, spike = facts[0:1, :1], facts[1:2, :1], facts[2:3, :1]
    for b in range(8):
        mean_t[:, b * 128 : b * 128 + 128] = cols[pl.ds(col_ids[b] & 7, 1), :] * per_row
        ident[:, b * 128 : b * 128 + 128] = lax.broadcasted_iota(jnp.int32, (1, 128), 1) + col_ids[b] * 128
    heavy[...] = jnp.zeros_like(heavy)
    for b in range(0, HEIGHT, STEP):
        cut = pl.ds(b, STEP)
        k_copies[b // STEP].wait()
        k = held[cut, :]
        blocks = range(b // 128, (b + STEP) // 128)
        r = jnp.concatenate([as_column(rows[i : i + 1, :] * per_row) for i in blocks])[:, :1]
        g = jnp.concatenate([lax.broadcasted_iota(jnp.int32, (128, 1), 0) + row_ids[i] * 128 for i in blocks])
        w = (slope * (k - r - mean_t[...]) + jnp.where(g == ident[...], base - spike, base)) * k
        wh[cut, :], wl[cut, :] = split(w)
        heavy[...] += jnp.sum(w.reshape(STEP // 8, 8, WIDTH), axis=0)
        load[cut, :] = jnp.broadcast_to(jnp.sum(w, axis=1, keepdims=True), (STEP, 128))
    for copy in copies:
        copy.wait()
    page_blocks([order[p] for p in FIRST], outs, wh, wl, load, ph, pl_, th, tl, 5)


def weigh(facts, row_ids, col_ids, order, kern, ph, pl_, th, tl, rows, cols):
    return pl.pallas_call(
        weight_kernel,
        out_shape=[pltpu.VMEM((SHARE, DEPTH), F32)] * 10
        + [pltpu.VMEM((HEIGHT, WIDTH), BF16), pltpu.VMEM((HEIGHT, WIDTH), BF16)]
        + [pltpu.VMEM((HEIGHT, 128), F32), jax.ShapeDtypeStruct((8, WIDTH), F32)]
        + [pltpu.VMEM((HEIGHT, DEPTH), BF16)] * 2
        + [pltpu.VMEM((WIDTH, DEPTH), BF16)] * 2,
        in_specs=[WHOLE] + [SCALAR] * 3 + [HBM] * 5 + [WHOLE] * 2,
        out_specs=[WHOLE] * 18,
        scratch_shapes=[
            pltpu.VMEM((1, WIDTH), F32),
            pltpu.VMEM((1, WIDTH), jnp.int32),
            pltpu.VMEM((HEIGHT, WIDTH), F32),
            pltpu.SemaphoreType.DMA((HEIGHT // STEP,)),
            pltpu.SemaphoreType.DMA((4,)),
        ],
        compiler_params=pltpu.CompilerParams(vmem_limit_bytes=22 * 2**20),
        cost_estimate=pl.CostEstimate(flops=10000, bytes_accessed=100000, transcendentals=0),
        name="weigh",
    )(facts, row_ids, col_ids, order, *map(afar, (kern, ph, pl_, th, tl)), rows, cols)


def page_kernel(*refs):
    order, wh, wl, load, ph, pl_, th, tl = refs[:8]
    page_blocks([order[p] for p in SECOND], refs[8:], wh, wl, load, ph, pl_, th, tl, 3)


def page_part(order, wh, wl, load, ph, pl_, th, tl):
    return pl.pallas_call(
        page_kernel,
        out_shape=[pltpu.VMEM((SHARE, DEPTH), F32)] * 6,
        in_specs=[SCALAR] + [WHOLE] * 7,
        out_specs=[WHOLE] * 6,
        compiler_params=pltpu.CompilerParams(vmem_limit_bytes=14 * 2**20),
        cost_estimate=pl.CostEstimate(flops=10000, bytes_accessed=100000, transcendentals=0),
        name="page_part",
    )(order, *map(near, (wh, wl, load, ph, pl_, th, tl)))


def text_kernel(start, heavy, wh, wl, ph, pl_, th, tl, *outs):
    load = jnp.sum(heavy[...], axis=0, keepdims=True)
    for j in range(start, start + 512, 256):
        folded = dot3(wh[:, j : j + 256], wl[:, j : j + 256], ph[...], pl_[...], TN)
        for i in range(2):
            q = j + i * 128
            t = th[q : q + 128, :].astype(F32) + tl[q : q + 128, :].astype(F32)
            column = as_column(load[:, q : q + 128])[:, :1]
            outs[(q - start) // 128][...] = folded[i * 128 : i * 128 + 128] - column * t


def text_part(start, heavy, wh, wl, ph, pl_, th, tl):
    return pl.pallas_call(
        functools.partial(text_kernel, start),
        out_shape=[pltpu.VMEM((SHARE, DEPTH), F32)] * 4,
        in_specs=[WHOLE] * 7,
        out_specs=[WHOLE] * 4,
        compiler_params=pltpu.CompilerParams(vmem_limit_bytes=14 * 2**20),
        cost_estimate=pl.CostEstimate(flops=10000, bytes_accessed=100000, transcendentals=0),
        name="text_part",
    )(heavy, *map(near, (wh, wl, ph, pl_, th, tl)))


def line_sum(x):
    return jnp.sum(x, axis=0, keepdims=True)


def without_mean(x):
    return x - jnp.mean(x)


def row_merge(size, r, r_got, r_out):
    d = r[:16] - r_got[:16]
    r_out[...] = r[...] + r_got[...]
    r_out[16:17] += line_sum(d * d) / (2.0 * size * WIDTH)


def column_merge(size, c, c_got, c_out):
    d = without_mean(c[:8] - c_got[:8])
    c_out[...] = c[...] + c_got[...]
    c_out[8:9] += line_sum(d * d) / (2.0 * size * HEIGHT)


def block_merge(size, u, u_got, u_out):
    d = u[1:2] - u_got[1:2]
    u_out[...] = u[...] + u_got[...]
    u_out[2:3] += d * d / (2.0 * size)


def row_facts(r, s_out):
    s_out[...] = jnp.zeros_like(s_out)
    s_out[0:2] = r[16:18]
    s_out[2:3] = line_sum(r[:16])


def block_facts(c, u_out):
    u_out[...] = jnp.zeros_like(u_out)
    u_out[0:1] = c[8:9]
    u_out[1:2] = jnp.broadcast_to(jnp.sum(c[:8]).reshape(1, 1), (1, 128))


def plain_merge(s, s_got, s_out):
    s_out[...] = s[...] + s_got[...]


def last_merge(s, u, facts):
    def whole(line):
        return jnp.broadcast_to(jnp.sum(line).reshape(1, 1), (1, 128))

    total = whole(s[2:3])
    frob_sq = whole(s[0:1] + u[0:1]) - u[2:3] / (COUNT * float(WIDTH))
    align = whole(s[1:2]) - total / COUNT
    grand = total / (float(COUNT) * COUNT)
    spike = 4.0 * COUNT / jnp.sqrt(frob_sq)
    slope = spike * (align / frob_sq)
    facts[...] = jnp.zeros_like(facts)
    facts[0:1] = slope
    facts[1:2] = slope * grand + spike / COUNT
    facts[2:3] = spike


def small(body, rows, *args):
    return pl.pallas_call(
        body,
        out_shape=jax.ShapeDtypeStruct((rows, 128), F32),
        in_specs=[WHOLE] * len(args),
        out_specs=WHOLE,
        compiler_params=pltpu.CompilerParams(vmem_limit_bytes=2**20),
        cost_estimate=pl.CostEstimate(flops=10000, bytes_accessed=100000, transcendentals=0),
        name="small",
    )(*args)


def from_pair(x, axis, bit):
    return lax.ppermute(x, axis, [(i, i ^ bit) for i in range(lax.axis_size(axis))])


def merged(body, size, x, got):
    return small(functools.partial(body, size), x.shape[0], x, got)


def statistics(r, c):
    r = merged(row_merge, 1, r, from_core(r))
    r_got, c_got = together(from_side(r), from_twin(c))
    r, c = merged(row_merge, 2, r, r_got), merged(column_merge, 1, c, c_got)
    r_got, c_got = together(from_pair(r, "y", 1), from_pair(c, "z", 1))
    r, c = merged(row_merge, 4, r, r_got), merged(column_merge, 2, c, c_got)
    r_got, c_got = together(from_pair(r, "y", 2), from_pair(c, "z", 2))
    r, c = merged(row_merge, 8, r, r_got), merged(column_merge, 4, c, c_got)
    s, u = small(row_facts, 8, r), small(block_facts, 8, c)
    u = merged(block_merge, 1, u, from_core(u))
    s_got, u_got = together(from_twin(s), from_side(u))
    s, u = small(plain_merge, 8, s, s_got), merged(block_merge, 2, u, u_got)
    s_got, u_got = together(from_pair(s, "z", 1), from_pair(u, "y", 1))
    s, u = small(plain_merge, 8, s, s_got), merged(block_merge, 4, u, u_got)
    s_got, u_got = together(from_pair(s, "z", 2), from_pair(u, "y", 2))
    s, u = small(plain_merge, 8, s, s_got), merged(block_merge, 8, u, u_got)
    return r, c, small(last_merge, 8, s, u)


def on_device(pages, transcripts, length_scale):
    spread_sq = length_scale[0] * length_scale[0]
    inverse = 0.5 / spread_sq
    z, xh, y, xl, core = (lax.axis_index(a) for a in AXES)
    blocks = lax.all_gather(pages, ("y", "xl", "core"), axis=0, tiled=True)
    texts = gather(transcripts)
    row_ids = (z * 2 + xh) * 16 + lax.iota(jnp.int32, 16)
    col_ids = jnp.stack(
        [
            (y * 4 + (xl ^ dq) * 2 + core) * 8 + ((z + dz) % 4) * 2 + (xh ^ dq)
            for dq in range(2)
            for dz in range(4)
        ]
    )
    order = jnp.stack(
        [
            ((y + dy) % 4) * 4 + (xl ^ dx) * 2 + (core ^ dc)
            for dc in range(2)
            for dx in range(2)
            for dy in range(4)
        ]
    )
    tnorm, th, tl = text_split(texts)
    kern, ph, pl_, r, c = cross(inverse.reshape(1), row_ids, col_ids, blocks, th, tl, tnorm)
    r, c, facts = statistics(r, c)
    *early, wh, wl, load, heavy, ph, pl_, th, tl = weigh(
        facts, row_ids, col_ids, order, kern, ph, pl_, th, tl, r, c
    )
    pages_ring, texts_ring = Ring("y", from_side), Ring("z", from_twin)
    o_up, o_down, o_far, far, other, heavy = together(
        *[early[i] + from_core(early[i + 5]) for i in range(5)], heavy
    )
    pages_ring.first(o_up, o_down, o_far)
    late = text_part(512, heavy, wh, wl, ph, pl_, th, tl)
    texts_ring.first(late[1], late[3], late[2])
    soon = text_part(0, together(heavy, *late)[0], wh, wl, ph, pl_, th, tl)
    *soon, order, g0, g1, g2 = together(*soon, order, *pages_ring.got)
    pages_ring.got = (g0, g1, g2)
    pages_ring.second(far, other)
    got = page_part(order, wh, wl, load, ph, pl_, th, tl)
    *got, g0, g1, g2, h0, h1, other = together(*got, *texts_ring.got, *pages_ring.halves, pages_ring.other)
    texts_ring.got, pages_ring.halves, pages_ring.other = (g0, g1, g2), (h0, h1), other
    up, down, own = together(*[got[i] + from_core(got[i + 3]) for i in range(3)])
    page_sum = pages_ring.third(own, up, down)
    texts_ring.second(soon[2], late[0])
    text_sum = texts_ring.third(soon[0], soon[1], soon[3])
    return (-page_sum / spread_sq, text_sum / spread_sq)


def solution(mesh):
    grid = Mesh(mesh.devices.reshape(SIZES), AXES)
    row, col = ("z", "xh"), ("y", "xl", "core")
    placed = (P(row + col, None), P(col + row, None), P())
    return jax.shard_map(
        on_device,
        mesh=grid,
        in_specs=placed,
        out_specs=(P(row + col, None), P(col + row, None)),
        check_vma=False,
    )
```

```python
import functools

import jax
import jax.numpy as jnp
from jax import lax
from jax.experimental import pallas as pl
from jax.experimental.pallas import tpu as pltpu
from jax.sharding import Mesh, PartitionSpec as P

AXES = ("z", "xh", "y", "xl", "core")
SIZES = (4, 2, 4, 2, 2)
COUNT = 16384
HEIGHT, WIDTH, DEPTH, SHARE = 2048, 1024, 1024, 128
F32, BF16 = jnp.float32, jnp.bfloat16
WHOLE = pl.BlockSpec(memory_space=pltpu.VMEM)
SCALAR = pl.BlockSpec(memory_space=pltpu.SMEM)
NT = (((1,), (1,)), ((), ()))
NN = (((1,), (0,)), ((), ()))
TN = (((0,), (0,)), ((), ()))


def from_next(x, axis, step):
    n = lax.axis_size(axis)
    return lax.ppermute(x, axis, [(i, (i - step) % n) for i in range(n)])


def from_twin(x):
    return lax.ppermute(x, ("xh", "xl"), [(0, 3), (3, 0), (1, 2), (2, 1)])


def from_side(x):
    return from_next(x, "xl", 1)


def from_core(x):
    return from_next(x, "core", 1)


def together(*values):
    return lax.optimization_barrier(values)


def gather(texts):
    half = texts.shape[0] // 2
    side, up, down = together(from_twin(texts), from_next(texts, "z", 1), from_next(texts, "z", -1))
    low, high = together(from_next(up[:half], "z", 1), from_next(down[half:], "z", -1))
    far = jnp.concatenate([low, high])
    side2, far2 = together(side, far)
    return [
        texts, up, far, down,
        side, from_next(side2, "z", 1), from_twin(far2), from_next(side2, "z", -1),
    ]


class Ring:
    def __init__(self, axis, across):
        self.axis, self.across = axis, across

    def first(self, o_up, o_down, o_far):
        self.got = (from_next(o_up, self.axis, -1), from_next(o_down, self.axis, 1), self.across(o_far))

    def second(self, far, other):
        low, high, o_far = self.got
        far = far + o_far
        half = far.shape[0] // 2
        self.halves = (from_next(far[:half], self.axis, -1), from_next(far[half:], self.axis, 1))
        self.other = self.across(other + low + high)

    def third(self, own, up, down):
        half = own.shape[0] // 2
        low, high = self.halves
        up = jnp.concatenate([up[:half] + low, up[half:]])
        down = jnp.concatenate([down[:half], down[half:] + high])
        return own + from_next(up, self.axis, -1) + from_next(down, self.axis, 1) + self.other


def split(x):
    high = x.astype(BF16)
    return high, (x - high.astype(F32)).astype(BF16)


def fold(x):
    return functools.reduce(jnp.add, [x[:, i : i + 128] for i in range(0, x.shape[1], 128)])


def as_lanes(x):
    return jnp.sum(jnp.transpose(fold(x)), axis=0, keepdims=True)


def as_column(line):
    return jnp.transpose(jnp.broadcast_to(line, (128, 128)))


def line_sum(x):
    return jnp.sum(x, axis=0, keepdims=True)


def dot3(ah, al, bh, bl, dims):
    d = functools.partial(lax.dot_general, dimension_numbers=dims, preferred_element_type=F32)
    return d(ah, bh) + (d(ah, bl) + d(al, bh))


CHUNK = 512
CHUNKS = HEIGHT // CHUNK
HBM = pl.BlockSpec(memory_space=pltpu.HBM)


def text_split_kernel(*refs):
    texts = refs[:8]
    tnorm, th_out, tl_out, th, tl, sem = refs[8:]
    for b in range(8):
        t = texts[b][...]
        cut = pl.ds(b * 128, 128)
        th[cut, :], tl[cut, :] = split(t)
        tnorm[:, b * 128 : b * 128 + 128] = as_lanes(t * t)
    high = pltpu.make_async_copy(th, th_out, sem.at[0])
    low = pltpu.make_async_copy(tl, tl_out, sem.at[1])
    high.start()
    low.start()
    high.wait()
    low.wait()


def text_split(texts):
    return pl.pallas_call(
        text_split_kernel,
        out_shape=[jax.ShapeDtypeStruct((1, WIDTH), F32)] + [pltpu.HBM((WIDTH, DEPTH), BF16)] * 2,
        in_specs=[WHOLE] * 8,
        out_specs=[WHOLE] + [HBM] * 2,
        scratch_shapes=[pltpu.VMEM((WIDTH, DEPTH), BF16)] * 2 + [pltpu.SemaphoreType.DMA((2,))],
        compiler_params=pltpu.CompilerParams(vmem_limit_bytes=14 * 2**20),
        cost_estimate=pl.CostEstimate(flops=2**24, bytes_accessed=8 * 2**20, transcendentals=0),
        name="text_split",
    )(*texts)


def cross_kernel(
    inverse_ref, row_ids, col_ids, pages, th_in, tl_in, tnorm,
    kern, ph, pl_, rows, cols,
    page_in, held, high, low, th, tl, col_acc, in_sem, out_sem, text_sem,
):
    inverse = inverse_ref[0]

    def page_copy(c):
        return pltpu.make_async_copy(pages.at[pl.ds(c * CHUNK, CHUNK), :], page_in.at[c % 2], in_sem.at[c])

    def out_copies(c):
        cut = pl.ds(c * CHUNK, CHUNK)
        return (
            pltpu.make_async_copy(high.at[c % 2], ph.at[cut, :], out_sem.at[0, c]),
            pltpu.make_async_copy(low.at[c % 2], pl_.at[cut, :], out_sem.at[1, c]),
            pltpu.make_async_copy(held.at[cut, :], kern.at[cut, :], out_sem.at[2, c]),
        )

    text_copies = (
        pltpu.make_async_copy(th_in, th, text_sem.at[0]),
        pltpu.make_async_copy(tl_in, tl, text_sem.at[1]),
    )
    text_copies = (
        pltpu.make_async_copy(th_in, th, text_sem.at[0]),
        pltpu.make_async_copy(tl_in, tl, text_sem.at[1]),
    )
    page_copy(0).start()
    for copy in text_copies:
        copy.start()
    page_copy(1).start()
    col_acc[...] = jnp.zeros_like(col_acc)
    rows[...] = jnp.zeros_like(rows)
    cols[...] = jnp.zeros_like(cols)
    for c in range(CHUNKS):
        page_copy(c).wait()
        h_copy, l_copy, k_copy = out_copies(c)
        if c >= 2:
            for copy in out_copies(c - 2)[:2]:
                copy.wait()
        p = page_in[c % 2]
        high[c % 2], low[c % 2] = split(p)
        pnorm = jnp.sum(p * p, axis=1, keepdims=True)
        h_copy.start()
        l_copy.start()
        if c + 2 < CHUNKS:
            page_copy(c + 2).start()
        if c == 0:
            for copy in text_copies:
                copy.wait()
        cross = dot3(high[c % 2], low[c % 2], th[...], tl[...], NT)
        k = jnp.exp((2.0 * cross - pnorm - tnorm[...]) * inverse)
        held[c * CHUNK : c * CHUNK + CHUNK, :] = k
        k_copy.start()
        col_acc[...] += jnp.sum(k.reshape(CHUNK // 8, 8, WIDTH), axis=0)
        for i in range(0, CHUNK, 128):
            line = (c * CHUNK + i) // 128
            rows[line : line + 1, :] = as_lanes(k[i : i + 128])

    total = jnp.sum(col_acc[...], axis=0, keepdims=True)
    for b in range(8):
        cols[pl.ds(col_ids[b] & 7, 1), :] = total[:, b * 128 : b * 128 + 128]
    tile_mean = jnp.sum(total) / (float(HEIGHT) * WIDTH)
    shift = total / float(HEIGHT) - tile_mean

    def stat(b, inner):
        k = held[pl.ds(pl.multiple_of(b * 128, 128), 128), :]
        mean = as_column(rows[pl.ds(b, 1), :] / float(WIDTH))[:, :1]
        own = k - mean - shift
        return inner + jnp.sum(fold(own * own).reshape(16, 8, 128), axis=0)

    inner = lax.fori_loop(0, 16, stat, jnp.zeros((8, 128), F32))
    rows[16:17, :] = jnp.sum(inner, axis=0, keepdims=True)
    diagonal = lax.broadcasted_iota(jnp.int32, (128, 128), 0) == lax.broadcasted_iota(jnp.int32, (128, 128), 1)
    for b in range(8):
        place = col_ids[b] - row_ids[0]

        @pl.when((place >= 0) & (place < 16))
        def _():
            k = held[pl.ds(pl.multiple_of(place * 128, 128), 128), b * 128 : b * 128 + 128]
            rows[17:18, :] += line_sum(jnp.where(diagonal, k, 0.0))

    for c in range(CHUNKS):
        for copy in out_copies(c)[0 if c >= CHUNKS - 2 else 2 :]:
            copy.wait()


def cross(inverse, row_ids, col_ids, pages, th, tl, tnorm):
    return pl.pallas_call(
        cross_kernel,
        out_shape=[
            pltpu.HBM((HEIGHT, WIDTH), F32),
            pltpu.HBM((HEIGHT, DEPTH), BF16),
            pltpu.HBM((HEIGHT, DEPTH), BF16),
            jax.ShapeDtypeStruct((24, 128), F32),
            jax.ShapeDtypeStruct((16, 128), F32),
        ],
        in_specs=[SCALAR] * 3 + [HBM] * 3 + [WHOLE],
        out_specs=[HBM] * 3 + [WHOLE] * 2,
        scratch_shapes=[
            pltpu.VMEM((2, CHUNK, DEPTH), F32),
            pltpu.VMEM((HEIGHT, WIDTH), F32),
            pltpu.VMEM((2, CHUNK, DEPTH), BF16),
            pltpu.VMEM((2, CHUNK, DEPTH), BF16),
            pltpu.VMEM((WIDTH, DEPTH), BF16),
            pltpu.VMEM((WIDTH, DEPTH), BF16),
            pltpu.VMEM((8, WIDTH), F32),
            pltpu.SemaphoreType.DMA((CHUNKS,)),
            pltpu.SemaphoreType.DMA((3, CHUNKS)),
            pltpu.SemaphoreType.DMA((2,)),
        ],
        compiler_params=pltpu.CompilerParams(vmem_limit_bytes=36 * 2**20),
        cost_estimate=pl.CostEstimate(flops=6 * 2**31, bytes_accessed=8 * 2**20, transcendentals=2**21),
        name="cross",
    )(inverse, row_ids, col_ids, afar(pages), afar(th), afar(tl), tnorm)


def afar(x):
    return pltpu.with_memory_space_constraint(x, pltpu.HBM)


def near(x):
    return pltpu.with_memory_space_constraint(x, pltpu.VMEM)


def block_at(place):
    return pl.ds(pl.multiple_of(place * 128, 128), 128)


def page_blocks(places, outs, wh, wl, load, ph, pl_, th, tl, size):
    for first in range(0, len(outs), size):
        cuts = [block_at(p) for p in places[first : first + size]]
        high = jnp.concatenate([wh[c, :] for c in cuts])
        low = jnp.concatenate([wl[c, :] for c in cuts])
        mixed = dot3(high, low, th[...], tl[...], NN)
        for i, c in enumerate(cuts):
            p = ph[c, :].astype(F32) + pl_[c, :].astype(F32)
            outs[first + i][...] = load[c, :1] * p - mixed[i * 128 : i * 128 + 128]


FIRST = (5, 7, 6, 2, 4, 13, 15, 14, 10, 12)
SECOND = (1, 3, 0, 9, 11, 8)
RUN = 5


def weight_kernel(*refs):
    facts, row_ids, col_ids, order, kern, ph_in, pl_in, th_in, tl_in, rows, cols = refs[:11]
    outs = refs[11:21]
    wh, wl, load, heavy, ph, pl_, th, tl = refs[21:29]
    mean_t, ident, held, high, low, k_sem, in_sem = refs[29:]
    places = [order[p] for p in FIRST + SECOND]
    k_copies = [
        pltpu.make_async_copy(kern.at[block_at(p), :], held.at[i], k_sem.at[i]) for i, p in enumerate(places)
    ]
    t_copies = [pltpu.make_async_copy(th_in, th, in_sem.at[0]), pltpu.make_async_copy(tl_in, tl, in_sem.at[1])]
    p_copies = [pltpu.make_async_copy(ph_in, ph, in_sem.at[2]), pltpu.make_async_copy(pl_in, pl_, in_sem.at[3])]
    for copy in k_copies[:RUN] + t_copies + k_copies[RUN : 2 * RUN] + p_copies + k_copies[2 * RUN :]:
        copy.start()
    per_row = 1.0 / COUNT
    slope, base, spike = facts[0:1, :1], facts[1:2, :1], facts[2:3, :1]
    for b in range(8):
        mean_t[:, b * 128 : b * 128 + 128] = cols[pl.ds(col_ids[b] & 7, 1), :] * per_row
        ident[:, b * 128 : b * 128 + 128] = lax.broadcasted_iota(jnp.int32, (1, 128), 1) + col_ids[b] * 128
    heavy[...] = jnp.zeros_like(heavy)

    def weights(i):
        p = places[i]
        k = held[i]
        r = as_column(rows[pl.ds(p, 1), :] * per_row)[:, :1]
        g = lax.broadcasted_iota(jnp.int32, (128, 1), 0) + row_ids[p] * 128
        w = (slope * (k - r - mean_t[...]) + jnp.where(g == ident[...], base - spike, base)) * k
        h, l = split(w)
        if i < 2 * RUN:
            high[i // RUN, i % RUN * 128 : i % RUN * 128 + 128] = h
            low[i // RUN, i % RUN * 128 : i % RUN * 128 + 128] = l
        cut = block_at(p)
        wh[cut, :] = h
        wl[cut, :] = l
        heavy[...] += jnp.sum(w.reshape(16, 8, WIDTH), axis=0)
        load[cut, :] = jnp.broadcast_to(jnp.sum(w, axis=1, keepdims=True), (128, 128))

    def product(run):
        mixed = dot3(high[run], low[run], th[...], tl[...], NN)
        for i in range(RUN):
            outs[run * RUN + i][...] = mixed[i * 128 : i * 128 + 128]

    def finish(run):
        for i in range(run * RUN, run * RUN + RUN):
            cut = block_at(places[i])
            p = ph[cut, :].astype(F32) + pl_[cut, :].astype(F32)
            outs[i][...] = load[cut, :1] * p - outs[i][...]

    for copy in k_copies[:RUN]:
        copy.wait()
    for i in range(RUN):
        weights(i)
    for copy in t_copies + k_copies[RUN : 2 * RUN]:
        copy.wait()
    product(0)
    for i in range(RUN, 2 * RUN):
        weights(i)
    for copy in p_copies + k_copies[2 * RUN :]:
        copy.wait()
    product(1)
    for i in range(2 * RUN, 16):
        weights(i)
    finish(0)
    finish(1)


def weigh(facts, row_ids, col_ids, order, kern, ph, pl_, th, tl, rows, cols):
    return pl.pallas_call(
        weight_kernel,
        out_shape=[pltpu.VMEM((SHARE, DEPTH), F32)] * 10
        + [pltpu.VMEM((HEIGHT, WIDTH), BF16), pltpu.VMEM((HEIGHT, WIDTH), BF16)]
        + [pltpu.VMEM((HEIGHT, 128), F32), jax.ShapeDtypeStruct((8, WIDTH), F32)]
        + [pltpu.VMEM((HEIGHT, DEPTH), BF16)] * 2
        + [pltpu.VMEM((WIDTH, DEPTH), BF16)] * 2,
        in_specs=[WHOLE] + [SCALAR] * 3 + [HBM] * 5 + [WHOLE] * 2,
        out_specs=[WHOLE] * 18,
        scratch_shapes=[
            pltpu.VMEM((1, WIDTH), F32),
            pltpu.VMEM((1, WIDTH), jnp.int32),
            pltpu.VMEM((16, 128, WIDTH), F32),
            pltpu.VMEM((2, RUN * 128, WIDTH), BF16),
            pltpu.VMEM((2, RUN * 128, WIDTH), BF16),
            pltpu.SemaphoreType.DMA((16,)),
            pltpu.SemaphoreType.DMA((4,)),
        ],
        compiler_params=pltpu.CompilerParams(vmem_limit_bytes=24 * 2**20),
        cost_estimate=pl.CostEstimate(flops=10000, bytes_accessed=100000, transcendentals=0),
        name="weigh",
    )(facts, row_ids, col_ids, order, *map(afar, (kern, ph, pl_, th, tl)), rows, cols)


def page_kernel(*refs):
    order, wh, wl, load, ph, pl_, th, tl = refs[:8]
    page_blocks([order[p] for p in SECOND], refs[8:], wh, wl, load, ph, pl_, th, tl, 3)


def page_part(order, wh, wl, load, ph, pl_, th, tl):
    return pl.pallas_call(
        page_kernel,
        out_shape=[pltpu.VMEM((SHARE, DEPTH), F32)] * 6,
        in_specs=[SCALAR] + [WHOLE] * 7,
        out_specs=[WHOLE] * 6,
        compiler_params=pltpu.CompilerParams(vmem_limit_bytes=14 * 2**20),
        cost_estimate=pl.CostEstimate(flops=10000, bytes_accessed=100000, transcendentals=0),
        name="page_part",
    )(order, *map(near, (wh, wl, load, ph, pl_, th, tl)))


def text_kernel(start, heavy, wh, wl, ph, pl_, th, tl, *outs):
    load = jnp.sum(heavy[...], axis=0, keepdims=True)
    for j in range(start, start + 512, 256):
        folded = dot3(wh[:, j : j + 256], wl[:, j : j + 256], ph[...], pl_[...], TN)
        for i in range(2):
            q = j + i * 128
            t = th[q : q + 128, :].astype(F32) + tl[q : q + 128, :].astype(F32)
            column = as_column(load[:, q : q + 128])[:, :1]
            outs[(q - start) // 128][...] = folded[i * 128 : i * 128 + 128] - column * t


def text_part(start, heavy, wh, wl, ph, pl_, th, tl):
    return pl.pallas_call(
        functools.partial(text_kernel, start),
        out_shape=[pltpu.VMEM((SHARE, DEPTH), F32)] * 4,
        in_specs=[WHOLE] * 7,
        out_specs=[WHOLE] * 4,
        compiler_params=pltpu.CompilerParams(vmem_limit_bytes=14 * 2**20),
        cost_estimate=pl.CostEstimate(flops=10000, bytes_accessed=100000, transcendentals=0),
        name="text_part",
    )(heavy, *map(near, (wh, wl, ph, pl_, th, tl)))


def without_mean(x):
    return x - jnp.mean(x)


def row_merge(size, r, r_got, r_out):
    d = r[:16] - r_got[:16]
    r_out[...] = r[...] + r_got[...]
    r_out[16:17] += line_sum(d * d) / (2.0 * size * WIDTH)


def column_merge(size, c, c_got, c_out):
    d = without_mean(c[:8] - c_got[:8])
    c_out[...] = c[...] + c_got[...]
    c_out[8:9] += line_sum(d * d) / (2.0 * size * HEIGHT)


def block_merge(size, u, u_got, u_out):
    d = u[1:2] - u_got[1:2]
    u_out[...] = u[...] + u_got[...]
    u_out[2:3] += d * d / (2.0 * size)


def row_facts(r, s_out):
    s_out[...] = jnp.zeros_like(s_out)
    s_out[0:2] = r[16:18]
    s_out[2:3] = line_sum(r[:16])


def block_facts(c, u_out):
    u_out[...] = jnp.zeros_like(u_out)
    u_out[0:1] = c[8:9]
    u_out[1:2] = jnp.broadcast_to(jnp.sum(c[:8]).reshape(1, 1), (1, 128))


def plain_merge(s, s_got, s_out):
    s_out[...] = s[...] + s_got[...]


def last_merge(s, u, facts):
    def whole(line):
        return jnp.broadcast_to(jnp.sum(line).reshape(1, 1), (1, 128))

    total = whole(s[2:3])
    frob_sq = whole(s[0:1] + u[0:1]) - u[2:3] / (COUNT * float(WIDTH))
    align = whole(s[1:2]) - total / COUNT
    grand = total / (float(COUNT) * COUNT)
    spike = 4.0 * COUNT / jnp.sqrt(frob_sq)
    slope = spike * (align / frob_sq)
    facts[...] = jnp.zeros_like(facts)
    facts[0:1] = slope
    facts[1:2] = slope * grand + spike / COUNT
    facts[2:3] = spike


def small(body, rows, *args):
    return pl.pallas_call(
        body,
        out_shape=jax.ShapeDtypeStruct((rows, 128), F32),
        in_specs=[WHOLE] * len(args),
        out_specs=WHOLE,
        compiler_params=pltpu.CompilerParams(vmem_limit_bytes=2**20),
        cost_estimate=pl.CostEstimate(flops=10000, bytes_accessed=100000, transcendentals=0),
        name="small",
    )(*args)


def from_pair(x, axis, bit):
    return lax.ppermute(x, axis, [(i, i ^ bit) for i in range(lax.axis_size(axis))])


def merged(body, size, x, got):
    return small(functools.partial(body, size), x.shape[0], x, got)


def statistics(r, c):
    r = merged(row_merge, 1, r, from_core(r))
    r_got, c_got = together(from_side(r), from_twin(c))
    r, c = merged(row_merge, 2, r, r_got), merged(column_merge, 1, c, c_got)
    r_got, c_got = together(from_pair(r, "y", 1), from_pair(c, "z", 1))
    r, c = merged(row_merge, 4, r, r_got), merged(column_merge, 2, c, c_got)
    r_got, c_got = together(from_pair(r, "y", 3), from_pair(c, "z", 3))
    r, c = merged(row_merge, 8, r, r_got), merged(column_merge, 4, c, c_got)
    s, u = small(row_facts, 8, r), small(block_facts, 8, c)
    u = merged(block_merge, 1, u, from_core(u))
    s_got, u_got = together(from_twin(s), from_side(u))
    s, u = small(plain_merge, 8, s, s_got), merged(block_merge, 2, u, u_got)
    s_got, u_got = together(from_pair(s, "z", 1), from_pair(u, "y", 1))
    s, u = small(plain_merge, 8, s, s_got), merged(block_merge, 4, u, u_got)
    s_got, u_got = together(from_pair(s, "z", 3), from_pair(u, "y", 3))
    s, u = small(plain_merge, 8, s, s_got), merged(block_merge, 8, u, u_got)
    return r, c, small(last_merge, 8, s, u)


def on_device(pages, transcripts, length_scale):
    spread_sq = length_scale[0] * length_scale[0]
    inverse = 0.5 / spread_sq
    z, xh, y, xl, core = (lax.axis_index(a) for a in AXES)
    blocks = lax.all_gather(pages, ("y", "xl", "core"), axis=0, tiled=True)
    texts = gather(transcripts)
    row_ids = (z * 2 + xh) * 16 + lax.iota(jnp.int32, 16)
    col_ids = jnp.stack(
        [
            (y * 4 + (xl ^ dq) * 2 + core) * 8 + ((z + dz) % 4) * 2 + (xh ^ dq)
            for dq in range(2)
            for dz in range(4)
        ]
    )
    order = jnp.stack(
        [
            ((y + dy) % 4) * 4 + (xl ^ dx) * 2 + (core ^ dc)
            for dc in range(2)
            for dx in range(2)
            for dy in range(4)
        ]
    )
    tnorm, th, tl = text_split(texts)
    kern, ph, pl_, r, c = cross(inverse.reshape(1), row_ids, col_ids, blocks, th, tl, tnorm)
    r, c, facts = statistics(r, c)
    *early, wh, wl, load, heavy, ph, pl_, th, tl = weigh(
        facts, row_ids, col_ids, order, kern, ph, pl_, th, tl, r, c
    )
    pages_ring, texts_ring = Ring("y", from_side), Ring("z", from_twin)
    o_up, o_down, o_far, far, other = [early[i] + from_core(early[i + 5]) for i in range(5)]
    o_up, o_down, o_far, heavy = together(o_up, o_down, o_far, heavy)
    pages_ring.first(o_up, o_down, o_far)
    late = text_part(512, heavy, wh, wl, ph, pl_, th, tl)
    texts_ring.first(late[1], late[3], late[2])
    far, other, heavy, *late = together(far, other, heavy, *late)
    soon = text_part(0, heavy, wh, wl, ph, pl_, th, tl)
    *soon, order, g0, g1, g2 = together(*soon, order, *pages_ring.got)
    pages_ring.got = (g0, g1, g2)
    pages_ring.second(far, other)
    got = page_part(order, wh, wl, load, ph, pl_, th, tl)
    *got, g0, g1, g2, h0, h1, other = together(*got, *texts_ring.got, *pages_ring.halves, pages_ring.other)
    texts_ring.got, pages_ring.halves, pages_ring.other = (g0, g1, g2), (h0, h1), other
    up, down, own = together(*[got[i] + from_core(got[i + 3]) for i in range(3)])
    page_sum = pages_ring.third(own, up, down)
    texts_ring.second(soon[2], late[0])
    text_sum = texts_ring.third(soon[0], soon[1], soon[3])
    return (-page_sum / spread_sq, text_sum / spread_sq)


def solution(mesh):
    grid = Mesh(mesh.devices.reshape(SIZES), AXES)
    row, col = ("z", "xh"), ("y", "xl", "core")
    placed = (P(row + col, None), P(col + row, None), P())
    return jax.shard_map(
        on_device,
        mesh=grid,
        in_specs=placed,
        out_specs=(P(row + col, None), P(col + row, None)),
        check_vma=False,
    )
```

```python
import functools

import jax
import jax.numpy as jnp
from jax import lax
from jax.experimental import pallas as pl
from jax.experimental.pallas import tpu as pltpu
from jax.sharding import Mesh, PartitionSpec as P

AXES = ("z", "xh", "y", "xl", "core")
SIZES = (4, 2, 4, 2, 2)
COUNT = 16384
HEIGHT, WIDTH, DEPTH, SHARE = 2048, 1024, 1024, 128
F32, BF16 = jnp.float32, jnp.bfloat16
WHOLE = pl.BlockSpec(memory_space=pltpu.VMEM)
SCALAR = pl.BlockSpec(memory_space=pltpu.SMEM)
NT = (((1,), (1,)), ((), ()))
NN = (((1,), (0,)), ((), ()))
TN = (((0,), (0,)), ((), ()))


def from_next(x, axis, step):
    n = lax.axis_size(axis)
    return lax.ppermute(x, axis, [(i, (i - step) % n) for i in range(n)])


def from_twin(x):
    return lax.ppermute(x, ("xh", "xl"), [(0, 3), (3, 0), (1, 2), (2, 1)])


def from_side(x):
    return from_next(x, "xl", 1)


def from_core(x):
    return from_next(x, "core", 1)


def together(*values):
    return lax.optimization_barrier(values)


def gather(texts):
    half = texts.shape[0] // 2
    side, up, down = together(from_twin(texts), from_next(texts, "z", 1), from_next(texts, "z", -1))
    low, high = together(from_next(up[:half], "z", 1), from_next(down[half:], "z", -1))
    far = jnp.concatenate([low, high])
    side2, far2 = together(side, far)
    return [
        texts, up, far, down,
        side, from_next(side2, "z", 1), from_twin(far2), from_next(side2, "z", -1),
    ]


class Ring:
    def __init__(self, axis, across):
        self.axis, self.across = axis, across

    def first(self, o_up, o_down, o_far):
        self.got = (from_next(o_up, self.axis, -1), from_next(o_down, self.axis, 1), self.across(o_far))

    def second(self, far, other):
        low, high, o_far = self.got
        far = far + o_far
        half = far.shape[0] // 2
        self.halves = (from_next(far[:half], self.axis, -1), from_next(far[half:], self.axis, 1))
        self.other = self.across(other + low + high)

    def third(self, own, up, down):
        half = own.shape[0] // 2
        low, high = self.halves
        up = jnp.concatenate([up[:half] + low, up[half:]])
        down = jnp.concatenate([down[:half], down[half:] + high])
        return own + from_next(up, self.axis, -1) + from_next(down, self.axis, 1) + self.other


def split(x):
    high = x.astype(BF16)
    return high, (x - high.astype(F32)).astype(BF16)


def fold(x):
    return functools.reduce(jnp.add, [x[:, i : i + 128] for i in range(0, x.shape[1], 128)])


def as_lanes(x):
    return jnp.sum(jnp.transpose(fold(x)), axis=0, keepdims=True)


def as_column(line):
    return jnp.transpose(jnp.broadcast_to(line, (128, 128)))


def line_sum(x):
    return jnp.sum(x, axis=0, keepdims=True)


def dot3(ah, al, bh, bl, dims):
    d = functools.partial(lax.dot_general, dimension_numbers=dims, preferred_element_type=F32)
    return d(ah, bh) + (d(ah, bl) + d(al, bh))


CHUNK = 512
CHUNKS = HEIGHT // CHUNK
HBM = pl.BlockSpec(memory_space=pltpu.HBM)


def text_split_kernel(*refs):
    texts = refs[:8]
    tnorm, th_out, tl_out, th, tl, sem = refs[8:]
    for b in range(8):
        t = texts[b][...]
        cut = pl.ds(b * 128, 128)
        th[cut, :], tl[cut, :] = split(t)
        tnorm[:, b * 128 : b * 128 + 128] = as_lanes(t * t)
    high = pltpu.make_async_copy(th, th_out, sem.at[0])
    low = pltpu.make_async_copy(tl, tl_out, sem.at[1])
    high.start()
    low.start()
    high.wait()
    low.wait()


def text_split(texts):
    return pl.pallas_call(
        text_split_kernel,
        out_shape=[jax.ShapeDtypeStruct((1, WIDTH), F32)] + [pltpu.HBM((WIDTH, DEPTH), BF16)] * 2,
        in_specs=[WHOLE] * 8,
        out_specs=[WHOLE] + [HBM] * 2,
        scratch_shapes=[pltpu.VMEM((WIDTH, DEPTH), BF16)] * 2 + [pltpu.SemaphoreType.DMA((2,))],
        compiler_params=pltpu.CompilerParams(vmem_limit_bytes=14 * 2**20),
        cost_estimate=pl.CostEstimate(flops=2**24, bytes_accessed=8 * 2**20, transcendentals=0),
        name="text_split",
    )(*texts)


def cross_kernel(
    inverse_ref, row_ids, col_ids, pages, th_in, tl_in, tnorm,
    kern, ph, pl_, rows, cols,
    page_in, held, high, low, th, tl, col_acc, in_sem, out_sem, text_sem,
):
    inverse = inverse_ref[0]

    def page_copy(c):
        return pltpu.make_async_copy(pages.at[pl.ds(c * CHUNK, CHUNK), :], page_in.at[c % 2], in_sem.at[c])

    def out_copies(c):
        cut = pl.ds(c * CHUNK, CHUNK)
        return (
            pltpu.make_async_copy(high.at[c % 2], ph.at[cut, :], out_sem.at[0, c]),
            pltpu.make_async_copy(low.at[c % 2], pl_.at[cut, :], out_sem.at[1, c]),
            pltpu.make_async_copy(held.at[cut, :], kern.at[cut, :], out_sem.at[2, c]),
        )

    text_copies = (
        pltpu.make_async_copy(th_in, th, text_sem.at[0]),
        pltpu.make_async_copy(tl_in, tl, text_sem.at[1]),
    )
    text_copies = (
        pltpu.make_async_copy(th_in, th, text_sem.at[0]),
        pltpu.make_async_copy(tl_in, tl, text_sem.at[1]),
    )
    page_copy(0).start()
    for copy in text_copies:
        copy.start()
    page_copy(1).start()
    col_acc[...] = jnp.zeros_like(col_acc)
    rows[...] = jnp.zeros_like(rows)
    cols[...] = jnp.zeros_like(cols)
    for c in range(CHUNKS):
        page_copy(c).wait()
        h_copy, l_copy, k_copy = out_copies(c)
        if c >= 2:
            for copy in out_copies(c - 2)[:2]:
                copy.wait()
        p = page_in[c % 2]
        high[c % 2], low[c % 2] = split(p)
        pnorm = jnp.sum(p * p, axis=1, keepdims=True)
        h_copy.start()
        l_copy.start()
        if c + 2 < CHUNKS:
            page_copy(c + 2).start()
        if c == 0:
            for copy in text_copies:
                copy.wait()
        cross = dot3(high[c % 2], low[c % 2], th[...], tl[...], NT)
        k = jnp.exp((2.0 * cross - pnorm - tnorm[...]) * inverse)
        held[c * CHUNK : c * CHUNK + CHUNK, :] = k
        k_copy.start()
        col_acc[...] += jnp.sum(k.reshape(CHUNK // 8, 8, WIDTH), axis=0)
        for i in range(0, CHUNK, 128):
            line = (c * CHUNK + i) // 128
            rows[line : line + 1, :] = as_lanes(k[i : i + 128])

    total = jnp.sum(col_acc[...], axis=0, keepdims=True)
    for b in range(8):
        cols[pl.ds(col_ids[b] & 7, 1), :] = total[:, b * 128 : b * 128 + 128]
    tile_mean = jnp.sum(total) / (float(HEIGHT) * WIDTH)
    shift = total / float(HEIGHT) - tile_mean

    def stat(b, inner):
        k = held[pl.ds(pl.multiple_of(b * 128, 128), 128), :]
        mean = as_column(rows[pl.ds(b, 1), :] / float(WIDTH))[:, :1]
        own = k - mean - shift
        return inner + jnp.sum(fold(own * own).reshape(16, 8, 128), axis=0)

    inner = lax.fori_loop(0, 16, stat, jnp.zeros((8, 128), F32))
    rows[16:17, :] = jnp.sum(inner, axis=0, keepdims=True)
    diagonal = lax.broadcasted_iota(jnp.int32, (128, 128), 0) == lax.broadcasted_iota(jnp.int32, (128, 128), 1)
    for b in range(8):
        place = col_ids[b] - row_ids[0]

        @pl.when((place >= 0) & (place < 16))
        def _():
            k = held[pl.ds(pl.multiple_of(place * 128, 128), 128), b * 128 : b * 128 + 128]
            rows[17:18, :] += line_sum(jnp.where(diagonal, k, 0.0))

    for c in range(CHUNKS):
        for copy in out_copies(c)[0 if c >= CHUNKS - 2 else 2 :]:
            copy.wait()


def cross(inverse, row_ids, col_ids, pages, th, tl, tnorm):
    return pl.pallas_call(
        cross_kernel,
        out_shape=[
            pltpu.HBM((HEIGHT, WIDTH), F32),
            pltpu.HBM((HEIGHT, DEPTH), BF16),
            pltpu.HBM((HEIGHT, DEPTH), BF16),
            jax.ShapeDtypeStruct((24, 128), F32),
            jax.ShapeDtypeStruct((16, 128), F32),
        ],
        in_specs=[SCALAR] * 3 + [HBM] * 3 + [WHOLE],
        out_specs=[HBM] * 3 + [WHOLE] * 2,
        scratch_shapes=[
            pltpu.VMEM((2, CHUNK, DEPTH), F32),
            pltpu.VMEM((HEIGHT, WIDTH), F32),
            pltpu.VMEM((2, CHUNK, DEPTH), BF16),
            pltpu.VMEM((2, CHUNK, DEPTH), BF16),
            pltpu.VMEM((WIDTH, DEPTH), BF16),
            pltpu.VMEM((WIDTH, DEPTH), BF16),
            pltpu.VMEM((8, WIDTH), F32),
            pltpu.SemaphoreType.DMA((CHUNKS,)),
            pltpu.SemaphoreType.DMA((3, CHUNKS)),
            pltpu.SemaphoreType.DMA((2,)),
        ],
        compiler_params=pltpu.CompilerParams(vmem_limit_bytes=36 * 2**20),
        cost_estimate=pl.CostEstimate(flops=6 * 2**31, bytes_accessed=8 * 2**20, transcendentals=2**21),
        name="cross",
    )(inverse, row_ids, col_ids, afar(pages), afar(th), afar(tl), tnorm)


def afar(x):
    return pltpu.with_memory_space_constraint(x, pltpu.HBM)


def near(x):
    return pltpu.with_memory_space_constraint(x, pltpu.VMEM)


def block_at(place):
    return pl.ds(pl.multiple_of(place * 128, 128), 128)


def page_blocks(places, outs, wh, wl, load, ph, pl_, th, tl, size):
    for first in range(0, len(outs), size):
        cuts = [block_at(p) for p in places[first : first + size]]
        high = jnp.concatenate([wh[c, :] for c in cuts])
        low = jnp.concatenate([wl[c, :] for c in cuts])
        mixed = dot3(high, low, th[...], tl[...], NN)
        for i, c in enumerate(cuts):
            p = ph[c, :].astype(F32) + pl_[c, :].astype(F32)
            outs[first + i][...] = load[c, :1] * p - mixed[i * 128 : i * 128 + 128]


FIRST = (5, 7, 6, 2, 4, 13, 15, 14, 10, 12)
SECOND = (1, 3, 0, 9, 11, 8)
RUN = 5


def weight_kernel(*refs):
    facts, row_ids, col_ids, order, kern, ph_in, pl_in, th_in, tl_in, rows, cols = refs[:11]
    outs = refs[11:21]
    wh, wl, load, heavy, ph, pl_, th, tl = refs[21:29]
    mean_t, ident, held, high, low, k_sem, in_sem = refs[29:]
    places = [order[p] for p in FIRST + SECOND]
    k_copies = [
        pltpu.make_async_copy(kern.at[block_at(p), :], held.at[i], k_sem.at[i]) for i, p in enumerate(places)
    ]
    t_copies = [pltpu.make_async_copy(th_in, th, in_sem.at[0]), pltpu.make_async_copy(tl_in, tl, in_sem.at[1])]
    p_copies = [pltpu.make_async_copy(ph_in, ph, in_sem.at[2]), pltpu.make_async_copy(pl_in, pl_, in_sem.at[3])]
    for copy in k_copies[:RUN] + t_copies + k_copies[RUN : 2 * RUN] + p_copies + k_copies[2 * RUN :]:
        copy.start()
    per_row = 1.0 / COUNT
    slope, base, spike = facts[0:1, :1], facts[1:2, :1], facts[2:3, :1]
    for b in range(8):
        mean_t[:, b * 128 : b * 128 + 128] = cols[pl.ds(col_ids[b] & 7, 1), :] * per_row
        ident[:, b * 128 : b * 128 + 128] = lax.broadcasted_iota(jnp.int32, (1, 128), 1) + col_ids[b] * 128
    heavy[...] = jnp.zeros_like(heavy)

    def weights(i):
        p = places[i]
        k = held[i]
        r = as_column(rows[pl.ds(p, 1), :] * per_row)[:, :1]
        g = lax.broadcasted_iota(jnp.int32, (128, 1), 0) + row_ids[p] * 128
        w = (slope * (k - r - mean_t[...]) + jnp.where(g == ident[...], base - spike, base)) * k
        h, l = split(w)
        if i < 2 * RUN:
            high[i // RUN, i % RUN * 128 : i % RUN * 128 + 128] = h
            low[i // RUN, i % RUN * 128 : i % RUN * 128 + 128] = l
        cut = block_at(p)
        wh[cut, :] = h
        wl[cut, :] = l
        heavy[...] += jnp.sum(w.reshape(16, 8, WIDTH), axis=0)
        load[cut, :] = jnp.broadcast_to(jnp.sum(w, axis=1, keepdims=True), (128, 128))

    def product(run):
        mixed = dot3(high[run], low[run], th[...], tl[...], NN)
        for i in range(RUN):
            outs[run * RUN + i][...] = mixed[i * 128 : i * 128 + 128]

    def finish(run):
        for i in range(run * RUN, run * RUN + RUN):
            cut = block_at(places[i])
            p = ph[cut, :].astype(F32) + pl_[cut, :].astype(F32)
            outs[i][...] = load[cut, :1] * p - outs[i][...]

    for copy in k_copies[:RUN]:
        copy.wait()
    for i in range(RUN):
        weights(i)
    for copy in t_copies + k_copies[RUN : 2 * RUN]:
        copy.wait()
    product(0)
    for i in range(RUN, 2 * RUN):
        weights(i)
    for copy in p_copies + k_copies[2 * RUN :]:
        copy.wait()
    product(1)
    for i in range(2 * RUN, 16):
        weights(i)
    finish(0)
    finish(1)


def weigh(facts, row_ids, col_ids, order, kern, ph, pl_, th, tl, rows, cols):
    return pl.pallas_call(
        weight_kernel,
        out_shape=[pltpu.VMEM((SHARE, DEPTH), F32)] * 10
        + [pltpu.VMEM((HEIGHT, WIDTH), BF16), pltpu.VMEM((HEIGHT, WIDTH), BF16)]
        + [pltpu.VMEM((HEIGHT, 128), F32), jax.ShapeDtypeStruct((8, WIDTH), F32)]
        + [pltpu.VMEM((HEIGHT, DEPTH), BF16)] * 2
        + [pltpu.VMEM((WIDTH, DEPTH), BF16)] * 2,
        in_specs=[WHOLE] + [SCALAR] * 3 + [HBM] * 5 + [WHOLE] * 2,
        out_specs=[WHOLE] * 18,
        scratch_shapes=[
            pltpu.VMEM((1, WIDTH), F32),
            pltpu.VMEM((1, WIDTH), jnp.int32),
            pltpu.VMEM((16, 128, WIDTH), F32),
            pltpu.VMEM((2, RUN * 128, WIDTH), BF16),
            pltpu.VMEM((2, RUN * 128, WIDTH), BF16),
            pltpu.SemaphoreType.DMA((16,)),
            pltpu.SemaphoreType.DMA((4,)),
        ],
        compiler_params=pltpu.CompilerParams(vmem_limit_bytes=24 * 2**20),
        cost_estimate=pl.CostEstimate(flops=10000, bytes_accessed=100000, transcendentals=0),
        name="weigh",
    )(facts, row_ids, col_ids, order, *map(afar, (kern, ph, pl_, th, tl)), rows, cols)


def page_kernel(*refs):
    order, wh, wl, load, ph, pl_, th, tl = refs[:8]
    page_blocks([order[p] for p in SECOND], refs[8:], wh, wl, load, ph, pl_, th, tl, 6)


def page_part(order, wh, wl, load, ph, pl_, th, tl):
    return pl.pallas_call(
        page_kernel,
        out_shape=[pltpu.VMEM((SHARE, DEPTH), F32)] * 6,
        in_specs=[SCALAR] + [WHOLE] * 7,
        out_specs=[WHOLE] * 6,
        compiler_params=pltpu.CompilerParams(vmem_limit_bytes=14 * 2**20),
        cost_estimate=pl.CostEstimate(flops=10000, bytes_accessed=100000, transcendentals=0),
        name="page_part",
    )(order, *map(near, (wh, wl, load, ph, pl_, th, tl)))


def text_kernel(start, heavy, wh, wl, ph, pl_, th, tl, *outs):
    load = jnp.sum(heavy[...], axis=0, keepdims=True)
    cut = slice(start, start + 512)
    folded = dot3(wh[:, cut], wl[:, cut], ph[...], pl_[...], TN)
    for i in range(4):
        q = start + i * 128
        t = th[q : q + 128, :].astype(F32) + tl[q : q + 128, :].astype(F32)
        column = as_column(load[:, q : q + 128])[:, :1]
        outs[i][...] = folded[i * 128 : i * 128 + 128] - column * t


def text_part(start, heavy, wh, wl, ph, pl_, th, tl):
    return pl.pallas_call(
        functools.partial(text_kernel, start),
        out_shape=[pltpu.VMEM((SHARE, DEPTH), F32)] * 4,
        in_specs=[WHOLE] * 7,
        out_specs=[WHOLE] * 4,
        compiler_params=pltpu.CompilerParams(vmem_limit_bytes=14 * 2**20),
        cost_estimate=pl.CostEstimate(flops=10000, bytes_accessed=100000, transcendentals=0),
        name="text_part",
    )(heavy, *map(near, (wh, wl, ph, pl_, th, tl)))


def without_mean(x):
    return x - jnp.mean(x)


def row_merge(size, r, r_got, r_out):
    d = r[:16] - r_got[:16]
    r_out[...] = r[...] + r_got[...]
    r_out[16:17] += line_sum(d * d) / (2.0 * size * WIDTH)


def column_merge(size, c, c_got, c_out):
    d = without_mean(c[:8] - c_got[:8])
    c_out[...] = c[...] + c_got[...]
    c_out[8:9] += line_sum(d * d) / (2.0 * size * HEIGHT)


def block_merge(size, u, u_got, u_out):
    d = u[1:2] - u_got[1:2]
    u_out[...] = u[...] + u_got[...]
    u_out[2:3] += d * d / (2.0 * size)


def row_facts(r, s_out):
    s_out[...] = jnp.zeros_like(s_out)
    s_out[0:2] = r[16:18]
    s_out[2:3] = line_sum(r[:16])


def block_facts(c, u_out):
    u_out[...] = jnp.zeros_like(u_out)
    u_out[0:1] = c[8:9]
    u_out[1:2] = jnp.broadcast_to(jnp.sum(c[:8]).reshape(1, 1), (1, 128))


def plain_merge(s, s_got, s_out):
    s_out[...] = s[...] + s_got[...]


def last_merge(s, u, facts):
    def whole(line):
        return jnp.broadcast_to(jnp.sum(line).reshape(1, 1), (1, 128))

    total = whole(s[2:3])
    frob_sq = whole(s[0:1] + u[0:1]) - u[2:3] / (COUNT * float(WIDTH))
    align = whole(s[1:2]) - total / COUNT
    grand = total / (float(COUNT) * COUNT)
    spike = 4.0 * COUNT / jnp.sqrt(frob_sq)
    slope = spike * (align / frob_sq)
    facts[...] = jnp.zeros_like(facts)
    facts[0:1] = slope
    facts[1:2] = slope * grand + spike / COUNT
    facts[2:3] = spike


def small(body, rows, *args):
    return pl.pallas_call(
        body,
        out_shape=jax.ShapeDtypeStruct((rows, 128), F32),
        in_specs=[WHOLE] * len(args),
        out_specs=WHOLE,
        compiler_params=pltpu.CompilerParams(vmem_limit_bytes=2**20),
        cost_estimate=pl.CostEstimate(flops=10000, bytes_accessed=100000, transcendentals=0),
        name="small",
    )(*args)


def from_pair(x, axis, bit):
    return lax.ppermute(x, axis, [(i, i ^ bit) for i in range(lax.axis_size(axis))])


def merged(body, size, x, got):
    return small(functools.partial(body, size), x.shape[0], x, got)


def statistics(r, c):
    c_got = from_twin(c)
    r_core, c = together(from_core(r), c)
    r = merged(row_merge, 1, r, r_core)
    r_got = from_side(r)
    r, c = merged(row_merge, 2, r, r_got), merged(column_merge, 1, c, c_got)
    r_got, c_got = (from_pair(r, "y", 1), from_pair(c, "z", 1))
    r, c = merged(row_merge, 4, r, r_got), merged(column_merge, 2, c, c_got)
    r_got, c_got = (from_pair(r, "y", 3), from_pair(c, "z", 3))
    r, c = merged(row_merge, 8, r, r_got), merged(column_merge, 4, c, c_got)
    s, u = small(row_facts, 8, r), small(block_facts, 8, c)
    u = merged(block_merge, 1, u, from_core(u))
    s_got, u_got = (from_twin(s), from_side(u))
    s, u = small(plain_merge, 8, s, s_got), merged(block_merge, 2, u, u_got)
    s_got, u_got = (from_pair(s, "z", 1), from_pair(u, "y", 1))
    s, u = small(plain_merge, 8, s, s_got), merged(block_merge, 4, u, u_got)
    s_got, u_got = (from_pair(s, "z", 3), from_pair(u, "y", 3))
    s, u = small(plain_merge, 8, s, s_got), merged(block_merge, 8, u, u_got)
    return r, c, small(last_merge, 8, s, u)


def on_device(pages, transcripts, length_scale):
    spread_sq = length_scale[0] * length_scale[0]
    inverse = 0.5 / spread_sq
    z, xh, y, xl, core = (lax.axis_index(a) for a in AXES)
    blocks = lax.all_gather(pages, ("y", "xl", "core"), axis=0, tiled=True)
    texts = gather(transcripts)
    row_ids = (z * 2 + xh) * 16 + lax.iota(jnp.int32, 16)
    col_ids = jnp.stack(
        [
            (y * 4 + (xl ^ dq) * 2 + core) * 8 + ((z + dz) % 4) * 2 + (xh ^ dq)
            for dq in range(2)
            for dz in range(4)
        ]
    )
    order = jnp.stack(
        [
            ((y + dy) % 4) * 4 + (xl ^ dx) * 2 + (core ^ dc)
            for dc in range(2)
            for dx in range(2)
            for dy in range(4)
        ]
    )
    tnorm, th, tl = text_split(texts)
    kern, ph, pl_, r, c = cross(inverse.reshape(1), row_ids, col_ids, blocks, th, tl, tnorm)
    r, c, facts = statistics(r, c)
    *early, wh, wl, load, heavy, ph, pl_, th, tl = weigh(
        facts, row_ids, col_ids, order, kern, ph, pl_, th, tl, r, c
    )
    pages_ring, texts_ring = Ring("y", from_side), Ring("z", from_twin)
    o_up, o_down, o_far, far, other = [early[i] + from_core(early[i + 5]) for i in range(5)]
    o_up, o_down, o_far, heavy = together(o_up, o_down, o_far, heavy)
    pages_ring.first(o_up, o_down, o_far)
    late = text_part(512, heavy, wh, wl, ph, pl_, th, tl)
    texts_ring.first(late[1], late[3], late[2])
    far, other, heavy, *late = together(far, other, heavy, *late)
    soon = text_part(0, heavy, wh, wl, ph, pl_, th, tl)
    *soon, order, g0, g1, g2 = together(*soon, order, *pages_ring.got)
    pages_ring.got = (g0, g1, g2)
    pages_ring.second(far, other)
    got = page_part(order, wh, wl, load, ph, pl_, th, tl)
    *got, g0, g1, g2, h0, h1, other = together(*got, *texts_ring.got, *pages_ring.halves, pages_ring.other)
    texts_ring.got, pages_ring.halves, pages_ring.other = (g0, g1, g2), (h0, h1), other
    up, down, own = together(*[got[i] + from_core(got[i + 3]) for i in range(3)])
    page_sum = pages_ring.third(own, up, down)
    texts_ring.second(soon[2], late[0])
    text_sum = texts_ring.third(soon[0], soon[1], soon[3])
    return (-page_sum / spread_sq, text_sum / spread_sq)


def solution(mesh):
    grid = Mesh(mesh.devices.reshape(SIZES), AXES)
    row, col = ("z", "xh"), ("y", "xl", "core")
    placed = (P(row + col, None), P(col + row, None), P())
    return jax.shard_map(
        on_device,
        mesh=grid,
        in_specs=placed,
        out_specs=(P(row + col, None), P(col + row, None)),
        check_vma=False,
    )
```
